32 devices in a mesh: dp: 16 (over z, y, x), mp: 2 (over core).
Axes of the slice: x: 2, y: 2, z: 4, core: 2. Of those that a mesh axis runs over, the one named last changes fastest.
Arguments:
- inputs: float32 [50176, 1024], P(('dp', 'mp')), may hold values from -6 to 6
- patch_keep: int32 [256, 196], P('dp'), may hold values from 0 to 1, as said below
- patch_gainone: float32 [1024], replicated, may hold values from 0.25 to 1.75
- patch_project: bfloat16 [3, 1024, 1024], P(None, None, 'mp'), may hold values from -0.1875 to 0.1875
- patch_outproj: bfloat16 [1024, 1024], P('mp'), may hold values from -1 to 1
- patch_gaintwo: float32 [1024], replicated, may hold values from 0.25 to 1.75
- patch_upward: bfloat16 [1024, 4096], P(None, 'mp'), may hold values from -0.1875 to 0.1875
- patch_downward: bfloat16 [4096, 1024], P('mp'), may hold values from -0.09375 to 0.09375
- learner_gain: float32 [1024], replicated, may hold values from 0.25 to 1.75
- learner_weight: float32 [1024, 8], replicated, may hold values from -0.375 to 0.375
- token_gainone: float32 [1024], replicated, may hold values from 0.25 to 1.75
- token_project: bfloat16 [3, 1024, 1024], P(None, None, 'mp'), may hold values from -0.1875 to 0.1875
- token_outproj: bfloat16 [1024, 1024], P('mp'), may hold values from -0.375 to 0.375
- token_gaintwo: float32 [1024], replicated, may hold values from 0.25 to 1.75
- token_upward: bfloat16 [1024, 4096], P(None, 'mp'), may hold values from -0.1875 to 0.1875
- token_downward: bfloat16 [4096, 1024], P('mp'), may hold values from -0.09375 to 0.09375
- output_grad: float32 [2048, 1024], P(('dp', 'mp')), may hold values from -6 to 6
Outputs:
- token_output: float32 [2048, 1024], P(('dp', 'mp'))
- input_grad: float32 [50176, 1024], P(('dp', 'mp'))
- patch_gainone_grad: float32 [1024], replicated
- patch_project_grad: float32 [3, 1024, 1024], P(None, None, 'mp')
- patch_outproj_grad: float32 [1024, 1024], P('mp')
- patch_gaintwo_grad: float32 [1024], replicated
- patch_upward_grad: float32 [1024, 4096], P(None, 'mp')
- patch_downward_grad: float32 [4096, 1024], P('mp')
- learner_gain_grad: float32 [1024], replicated
- learner_weight_grad: float32 [1024, 8], replicated
- token_gainone_grad: float32 [1024], replicated
- token_project_grad: float32 [3, 1024, 1024], P(None, None, 'mp')
- token_outproj_grad: float32 [1024, 1024], P('mp')
- token_gaintwo_grad: float32 [1024], replicated
- token_upward_grad: float32 [1024, 4096], P(None, 'mp')
- token_downward_grad: float32 [4096, 1024], P('mp')
The draws below stay inside these ranges and needn't reach their ends.
Inputs may be any that keep to these rules, and one draw needn't show every extreme that they name: `patch_keep`: each image keeps between 98 and 196 of its patches, the count and the kept places drawn afresh for every image.
All inputs are finite; a program needn't handle non-finite values.
Results may differ from the reference program's by a relative error of at most 0.03.
Values may be sent and summed in bfloat16 or wider, within the bound.
No kernel may reach another device: no remote copies, remote signals or barrier semaphores. Data moves between devices by JAX's collectives and lax.ppermute only.
A program may use at most 384 MiB of HBM per device.

```python
import jax
import jax.numpy as jnp
from jax import lax

D = 1024
HEADS = 16
HEAD_DIM = 64
FF = 4096
P_SIZE = 196
S = 8
IMAGES = 256


def draw_patch_keep(key, part):
    key = jax.random.fold_in(key, 1)
    count_key, order_key = jax.random.split(key)
    counts = jax.random.randint(count_key, (IMAGES,), P_SIZE // 2, P_SIZE + 1)
    orders = jax.vmap(lambda single: jax.random.permutation(single, P_SIZE))(jax.random.split(order_key, IMAGES))
    return (orders < counts[:, None]).astype(jnp.int32)


def steps_of(key, extent, cuts, least, largest):
    loudness, own = 1.0, jax.random.fold_in(key, 6)
    for axis_at, parts in cuts:
        steps = jnp.exp(jax.random.uniform(jax.random.fold_in(own, axis_at), (parts,), jnp.float32, least / len(cuts), largest / len(cuts)))
        loudness = loudness * jnp.repeat(steps, extent[axis_at] // parts).reshape([-1 if axis == axis_at else 1 for axis in range(len(extent))])
    return loudness


def bell_draw(stream_key, dims, width, reach, cuts=(), held_as=jnp.bfloat16):
    drawn = width * jax.random.normal(stream_key, dims, jnp.float32)
    if cuts:
        drawn = drawn * steps_of(stream_key, dims, cuts, -0.22, 0.18)
    return jnp.clip(drawn, -reach, reach).astype(held_as)


def setup_inputs(seed: int = 0) -> dict:
    key_list = jax.random.split(jax.random.key(seed), 18)
    return {
        "inputs": bell_draw(key_list[0], (IMAGES * P_SIZE, D), 1.0, 6.0, ((0, 32),), jnp.float32),
        "patch_keep": draw_patch_keep(jax.random.fold_in(key_list[17], 71), 0),
        "patch_gainone": jnp.clip(1.0 + 0.15 * jax.random.normal(key_list[2], (D,), jnp.float32), 0.25, 1.75),
        "patch_project": bell_draw(key_list[3], (3, D, D), D ** -0.5, 0.1875, ((2, 2),)),
        "patch_outproj": bell_draw(key_list[4], (D, D), (D // 32) ** -0.5, 1.0, ((0, 2),)),
        "patch_gaintwo": jnp.clip(1.0 + 0.15 * jax.random.normal(key_list[5], (D,), jnp.float32), 0.25, 1.75),
        "patch_upward": bell_draw(key_list[6], (D, FF), D ** -0.5, 0.1875, ((1, 2),)),
        "patch_downward": bell_draw(key_list[7], (FF, D), FF ** -0.5, 0.09375, ((0, 2),)),
        "learner_gain": jnp.clip(1.0 + 0.15 * jax.random.normal(key_list[8], (D,), jnp.float32), 0.25, 1.75),
        "learner_weight": bell_draw(key_list[9], (D, S), (D // 4) ** -0.5, 0.375, (), jnp.float32),
        "token_gainone": jnp.clip(1.0 + 0.15 * jax.random.normal(key_list[10], (D,), jnp.float32), 0.25, 1.75),
        "token_project": bell_draw(key_list[11], (3, D, D), D ** -0.5, 0.1875, ((2, 2),)),
        "token_outproj": bell_draw(key_list[12], (D, D), (D // 4) ** -0.5, 0.375, ((0, 2),)),
        "token_gaintwo": jnp.clip(1.0 + 0.15 * jax.random.normal(key_list[13], (D,), jnp.float32), 0.25, 1.75),
        "token_upward": bell_draw(key_list[14], (D, FF), D ** -0.5, 0.1875, ((1, 2),)),
        "token_downward": bell_draw(key_list[15], (FF, D), FF ** -0.5, 0.09375, ((0, 2),)),
        "output_grad": bell_draw(key_list[16], (IMAGES * S, D), 1.0, 6.0, ((0, 32),), jnp.float32),
    }


@jax.custom_vjp
def low(v):
    return lax.optimization_barrier(v.astype(jnp.bfloat16)).astype(jnp.float32)

@jax.custom_vjp
def low_back(v):
    return v

def low_keep(v):
    return (low(v), None)

def low_pass(kept, grad):
    return (grad,)

def back_keep(v):
    return (v, None)

def back_low(kept, grad):
    return (low(grad),)
low.defvjp(low_keep, low_pass)
low_back.defvjp(back_keep, back_low)
epsilon = 1e-06
highest = lax.Precision.HIGHEST

def norm_rows(matrix, scales):
    center = matrix - lax.optimization_barrier(jnp.mean(matrix, axis=-1, keepdims=True))
    spread = lax.optimization_barrier(jnp.mean(center * center, axis=-1, keepdims=True))
    return center * lax.rsqrt(spread + epsilon) * scales

def block(inputs, params, visible):
    gain_one, weight_qkv, weight_out, gain_two, weight_up, weight_down = params
    groups, length = (inputs.shape[0], inputs.shape[1])
    across = low(norm_rows(inputs, gain_one))
    projected = low(low_back(jnp.einsum('gld,tdc->tglc', across, weight_qkv, precision=highest)))
    head_shape = (groups, length, HEADS, HEAD_DIM)
    queries = projected[0].reshape(head_shape)
    key_rows = projected[1].reshape(head_shape)
    values = projected[2].reshape(head_shape)
    scores = low_back(jnp.einsum('gqhe,gkhe->ghqk', queries, key_rows, precision=highest) * HEAD_DIM ** (-0.5))
    scores = jnp.where(visible[:, None, None, :], scores, -1e+30)
    probs = jax.nn.softmax(scores, axis=-1)
    attended = jnp.einsum('ghqk,gkhe->gqhe', low(probs), values, precision=highest)
    attended = low(low_back(attended.reshape(groups, length, HEADS * HEAD_DIM)))
    hidden = inputs + low_back(jnp.einsum('gld,de->gle', attended, weight_out, precision=highest))
    second = low(norm_rows(hidden, gain_two))
    upward = low_back(jnp.einsum('gld,df->glf', second, weight_up, precision=highest))
    active = low(jax.nn.gelu(upward, approximate=False))
    return hidden + low_back(jnp.einsum('glf,fd->gld', active, weight_down, precision=highest))

def learn(outputs, gain, weight, visible):
    normed = norm_rows(outputs, gain)
    logits = jnp.einsum('gpd,ds->gps', normed, weight, precision=highest)
    logits = jnp.where(visible[:, :, None], logits, -1e+30)
    shares = jax.nn.softmax(logits, axis=1)
    return jnp.einsum('gps,gpd->gsd', shares, outputs, precision=highest)

def reference(inputs, patch_keep, patch_gainone, patch_project, patch_outproj, patch_gaintwo, patch_upward, patch_downward, learner_gain, learner_weight, token_gainone, token_project, token_outproj, token_gaintwo, token_upward, token_downward, output_grad):
    lower = tuple((tensor.astype(jnp.float32) for tensor in (patch_gainone, patch_project, patch_outproj, patch_gaintwo, patch_upward, patch_downward)))
    upper = tuple((tensor.astype(jnp.float32) for tensor in (token_gainone, token_project, token_outproj, token_gaintwo, token_upward, token_downward)))
    learner = (learner_gain.astype(jnp.float32), learner_weight.astype(jnp.float32))
    visible = patch_keep > 0

    def whole(inputs_f, lower_p, learn_p, upper_p):
        group_inputs = inputs_f.reshape(IMAGES // 8, 8, P_SIZE, D)
        group_visible = visible.reshape(IMAGES // 8, 8, P_SIZE)

        def one_group(paired):
            portion, seen = paired
            patched = block(portion, lower_p, seen)
            tokens = learn(patched, learn_p[0], learn_p[1], seen)
            return block(tokens, upper_p, jnp.ones((8, S), dtype=jnp.bool_))
        mapped = lax.map(jax.checkpoint(one_group), (group_inputs, group_visible))
        return mapped.reshape(IMAGES * S, D)
    result, pull = jax.vjp(whole, inputs.astype(jnp.float32), lower, learner, upper)
    grad_inputs, grad_lower, grad_learn, grad_upper = pull(output_grad.astype(jnp.float32))
    return (result, grad_inputs, grad_lower[0], grad_lower[1], grad_lower[2], grad_lower[3], grad_lower[4], grad_lower[5], grad_learn[0], grad_learn[1], grad_upper[0], grad_upper[1], grad_upper[2], grad_upper[3], grad_upper[4], grad_upper[5])
```

```python
import math
from functools import partial

import jax
import jax.numpy as jnp
from jax import lax
from jax.experimental import pallas as pl
from jax.experimental.pallas import tpu as pltpu
from jax.sharding import PartitionSpec as P

HEAD_DIM = 64
P_SIZE = 196
S = 8


epsilon = 1e-06
highest = lax.Precision.HIGHEST


WINDOW = 208


def key_bias(keep):
    pieces = []
    for place in range(keep.shape[0]):
        offset = place * P_SIZE % 16
        row = jnp.where(keep[place], 0.0, -1e30).astype(jnp.float32)
        pieces.append(jnp.pad(row, (offset, WINDOW - P_SIZE - offset), constant_values=-1e30))
    return jnp.stack(pieces)[:, :, None]


def nt(left, right):
    return lax.dot_general(
        left, right, (((1,), (1,)), ((), ())), preferred_element_type=jnp.float32
    )


def mm(left, right):
    return jnp.dot(left, right, preferred_element_type=jnp.float32)


def only(head, tensor):
    lane = lax.broadcasted_iota(jnp.int32, tensor.shape, 1)
    return jnp.where((lane < HEAD_DIM) == (head == 0), tensor, jnp.zeros_like(tensor))


def pick(pair):
    lane = lax.broadcasted_iota(jnp.int32, pair[0].shape, 1)
    return jnp.where(lane < HEAD_DIM, pair[0], pair[1])


def mix(query, keys, values, bias):
    turned = values.T
    pieces = []
    for head in range(2):
        scores = nt(only(head, keys), query) + bias
        weights = jnp.exp(scores - jnp.max(scores, axis=0, keepdims=True))
        total = jnp.sum(weights, axis=0, keepdims=True)
        mixed = mm(turned[head * HEAD_DIM : (head + 1) * HEAD_DIM], weights.astype(jnp.bfloat16))
        pieces.append(mixed * (1.0 / total))
    return jnp.concatenate(pieces, axis=0).T.astype(jnp.bfloat16)


def mix_back(query, keys, values, grad, bias):
    turned = keys.T
    by_query, by_key, by_value = [], [], []
    for head in range(2):
        scores = nt(only(head, keys), query) + bias
        weights = jnp.exp(scores - jnp.max(scores, axis=0, keepdims=True))
        total = jnp.sum(weights, axis=0, keepdims=True)
        shares = weights * (1.0 / total)
        product = shares * nt(only(head, values), grad)
        inner = jnp.sum(product, axis=0, keepdims=True)
        grad_scores = (product - shares * inner).astype(jnp.bfloat16)
        by_value.append(mm(shares.astype(jnp.bfloat16), grad))
        by_key.append(mm(grad_scores, query))
        by_query.append(mm(turned[head * HEAD_DIM : (head + 1) * HEAD_DIM], grad_scores))
    grad_query = jnp.concatenate(by_query, axis=0).T * HEAD_DIM**-0.5
    return tuple(value.astype(jnp.bfloat16) for value in (grad_query, pick(by_key), pick(by_value)))


def scaled(query):
    return query * jnp.bfloat16(HEAD_DIM**-0.5)


def window_of(place):
    first = place * P_SIZE
    start = first // 16 * 16
    row = lax.broadcasted_iota(jnp.int32, (WINDOW, 2 * HEAD_DIM), 0)
    offset = first - start
    return pl.ds(start, WINDOW), (row >= offset) & (row < offset + P_SIZE)


def attend_kernel(images, bias_ref, qkv_ref, out_ref):
    for place in range(images):
        window, inside = window_of(place)
        mixed = mix(
            scaled(qkv_ref[0, window, :]),
            qkv_ref[1, window, :],
            qkv_ref[2, window, :],
            bias_ref[place],
        )
        out_ref[window, :] = jnp.where(inside, mixed, out_ref[window, :])


def attend_back_kernel(images, bias_ref, qkv_ref, grad_ref, out_ref):
    for place in range(images):
        window, inside = window_of(place)
        grad = grad_ref[window, :]
        parts = mix_back(
            scaled(qkv_ref[0, window, :]),
            qkv_ref[1, window, :],
            qkv_ref[2, window, :],
            jnp.where(inside, grad, jnp.zeros_like(grad)),
            bias_ref[place],
        )
        for at, value in enumerate(parts):
            out_ref[at, window, :] = jnp.where(inside, value, out_ref[at, window, :])


def attention(kernel, bias, projected, grads, panel, panels):
    rows, columns = projected.shape[1:]
    spare = -rows % 16
    if spare:
        projected = jnp.pad(projected, ((0, 0), (0, spare), (0, 0)))
        grads = [jnp.pad(grad, ((0, spare), (0, 0))) for grad in grads]
    wide, columns = 2 * HEAD_DIM, columns // panels
    pairs = columns // wide
    first = panel * pairs
    rows += spare
    plane = pl.BlockSpec((rows, wide), lambda pair: (0, pair))
    triple = pl.BlockSpec((3, rows, wide), lambda pair: (0, 0, pair))
    shape = (rows, columns)
    out = pl.pallas_call(
        kernel,
        grid=(pairs,),
        in_specs=[
            pl.BlockSpec(bias.shape, lambda pair: (0,) * bias.ndim),
            pl.BlockSpec((3, rows, wide), lambda pair: (0, 0, first + pair)),
        ]
        + [pl.BlockSpec((rows, wide), lambda pair: (0, first + pair))] * len(grads),
        out_specs=triple if grads else plane,
        out_shape=jax.ShapeDtypeStruct((3,) + shape if grads else shape, jnp.bfloat16),
        compiler_params=params(14),
        cost_estimate=light(),
        name="attend_back" if grads else "attend",
    )(bias, projected, *grads)
    return out[..., : rows - spare, :] if spare else out


def attend(bias, projected):
    return attention(partial(attend_kernel, bias.shape[0]), bias, projected, [], 0, 1)


def attend_back(bias, projected, grad_context, panel, panels):
    kernel = partial(attend_back_kernel, bias.shape[0])
    return attention(kernel, bias, projected, [grad_context], panel, panels)


def tn(left, right):
    return lax.dot_general(
        left, right, (((0,), (0,)), ((), ())), preferred_element_type=jnp.float32
    )


def row_mean(matrix):
    width = matrix.shape[1]
    folded = matrix[:, :128]
    for at in range(128, width, 128):
        folded = folded + matrix[:, at : at + 128]
    return jnp.sum(folded, axis=-1, keepdims=True) * (1.0 / width)


def standard(matrix):
    center = matrix - row_mean(matrix)
    spread = row_mean(center * center)
    inverse = lax.rsqrt(spread + epsilon)
    return center * inverse, inverse


def standard_back(grad, normal, inverse, gain):
    scaled_grad = grad * gain
    mean = row_mean(scaled_grad)
    along = row_mean(scaled_grad * normal)
    return (
        inverse * (scaled_grad - mean - normal * along),
        jnp.sum((grad * normal).reshape(-1, 8, grad.shape[1]), axis=0),
    )


def gelu_pair(upward):
    bell = jnp.exp(upward * upward * -0.5)
    base = 1.0 + jnp.abs(upward) * (0.3275911 * 0.5**0.5)
    ratio = pl.reciprocal(base, approx=True)
    ratio = ratio * (2.0 - base * ratio)
    series = 0.5 * 1.061405429
    for factor in (-1.453152027, 1.421413741, -0.284496736, 0.254829592):
        series = series * ratio + 0.5 * factor
    tail = series * ratio * bell
    below = jnp.where(upward < 0.0, tail, 1.0 - tail)
    slope = below + upward * bell * (0.5 / math.pi) ** 0.5
    return (upward * below).astype(jnp.bfloat16), slope.astype(jnp.bfloat16)


def spans(rows, most):
    if rows <= most or rows % 16:
        return [(0, rows)]
    parts = -(-rows // most)
    cuts = [rows // 16 * at // parts * 16 for at in range(parts + 1)]
    return list(zip(cuts, cuts[1:]))


def row_block(rows, most):
    for count in range(1, rows + 1):
        if rows % count == 0 and rows // count <= most and rows // count % 16 == 0:
            return rows // count
    return rows


def by_rows(rows, work, step=112):
    size = row_block(rows, 128)

    def run(first):
        for at in range(0, size, step):
            start = first + at
            if not isinstance(start, int):
                start = pl.multiple_of(start, 16)
            work(pl.ds(start, min(step, size - at)))

    if size == rows:
        run(0)
        return

    def one(at, carry):
        run(at * size)
        return carry

    lax.fori_loop(0, rows // size, one, 0)


def light():
    return pl.CostEstimate(flops=1000, bytes_accessed=1000, transcendentals=0)


def params(mebibytes):
    return pltpu.CompilerParams(vmem_limit_bytes=mebibytes * 1024 * 1024)


def eight_spec(width):
    return pl.BlockSpec((8, width), lambda *at: (0, 0))


def whole_spec(array):
    return pl.BlockSpec(array.shape, lambda *at: (0,) * array.ndim)


def norm_kernel(input_ref, gain_ref, out_ref):
    def work(rows):
        normal = standard(input_ref[rows, :])[0]
        out_ref[rows, :] = (normal * gain_ref[...]).astype(jnp.bfloat16)

    by_rows(input_ref.shape[0], work)


def norm(inputs, gain):
    rows, width = inputs.shape
    block = row_block(rows, 400)
    line = pl.BlockSpec((block, width), lambda at: (at, 0))
    gain = gain[None]
    return pl.pallas_call(
        norm_kernel,
        grid=(rows // block,),
        in_specs=[line, whole_spec(gain)],
        out_specs=line,
        out_shape=jax.ShapeDtypeStruct((rows, width), jnp.bfloat16),
        compiler_params=params(8),
        cost_estimate=light(),
        name="norm",
    )(inputs, gain)


def outward_kernel(shares, *refs):
    context_refs, weight_refs = refs[:shares], refs[shares : 2 * shares]
    input_ref, gain_ref, hidden_ref, second_ref = refs[2 * shares :]
    total = input_ref[...]
    for context_ref, weight_ref in zip(context_refs, weight_refs):
        total = total + mm(context_ref[...], weight_ref[...])
    hidden_ref[...] = total

    def work(rows):
        normal = standard(hidden_ref[rows, :])[0]
        second_ref[rows, :] = (normal * gain_ref[...]).astype(jnp.bfloat16)

    by_rows(input_ref.shape[0], work)


def outward(contexts, weights, inputs, gain):
    rows, width = inputs.shape
    block = row_block(rows, 400)
    line = pl.BlockSpec((block, width), lambda at: (at, 0))
    gain = gain[None]
    heads = contexts[0].shape[1]
    return pl.pallas_call(
        partial(outward_kernel, len(contexts)),
        grid=(rows // block,),
        in_specs=[pl.BlockSpec((block, heads), lambda at: (at, 0))] * len(contexts)
        + [whole_spec(weight) for weight in weights]
        + [line, whole_spec(gain)],
        out_specs=[line, line],
        out_shape=[
            jax.ShapeDtypeStruct((rows, width), jnp.float32),
            jax.ShapeDtypeStruct((rows, width), jnp.bfloat16),
        ],
        compiler_params=params(16),
        cost_estimate=light(),
        name="outward",
    )(*contexts, *weights, inputs, gain)


def ff_kernel(shares, per, *refs):
    second_ref, hidden_ref = refs[:2]
    up_refs, down_refs = refs[2 : 2 + shares], refs[2 + shares : 2 + 2 * shares]
    result_ref = refs[2 + 2 * shares]
    active_refs, slope_refs = refs[3 + 2 * shares : 3 + 3 * shares], refs[3 + 3 * shares :]
    chunk = pl.program_id(1)

    @pl.when(chunk == 0)
    def _():
        result_ref[...] = hidden_ref[...]

    for share in range(shares):

        @pl.when((chunk >= share * per) & (chunk < (share + 1) * per))
        def _():
            ranges = spans(second_ref.shape[0], 400)
            up, down = up_refs[share][...], down_refs[share][...]
            ahead = mm(second_ref[ranges[0][0] : ranges[0][1], :], up)
            for at, (start, end) in enumerate(ranges):
                upward = ahead
                if at + 1 < len(ranges):
                    ahead = mm(second_ref[ranges[at + 1][0] : ranges[at + 1][1], :], up)
                active, slope = gelu_pair(upward)
                active_refs[share][start:end, :] = active
                slope_refs[share][start:end, :] = slope
                result_ref[start:end, :] += mm(active, down)


def share_spec(block, place, share, per):
    if place == 1:
        return pl.BlockSpec(block, lambda at, chunk: (0, jnp.clip(chunk - share * per, 0, per - 1)))
    if place == 0:
        return pl.BlockSpec(block, lambda at, chunk: (jnp.clip(chunk - share * per, 0, per - 1), 0))
    return pl.BlockSpec(block, lambda at, chunk: (at, jnp.clip(chunk - share * per, 0, per - 1)))


def ff_sizes(rows, ups, most):
    block = rows // 2 if rows % 32 == 0 and rows > 1024 else rows
    width, units = ups[0].shape
    size = min(most if rows > 128 else 1024, units)
    return block, width, units, size, units // size


def feed(second, hidden, ups, downs):
    rows, shares = second.shape[0], len(ups)
    block, width, units, size, per = ff_sizes(rows, ups, 1024)
    line = pl.BlockSpec((block, width), lambda at, chunk: (at, 0))
    piece = [share_spec((block, size), 2, share, per) for share in range(shares)]
    out = pl.pallas_call(
        partial(ff_kernel, shares, per),
        grid=(rows // block, shares * per),
        in_specs=[line, line]
        + [share_spec((width, size), 1, share, per) for share in range(shares)]
        + [share_spec((size, width), 0, share, per) for share in range(shares)],
        out_specs=[line] + piece + piece,
        out_shape=[jax.ShapeDtypeStruct((rows, width), jnp.float32)]
        + [jax.ShapeDtypeStruct((rows, units), jnp.bfloat16)] * (2 * shares),
        compiler_params=params(56),
        cost_estimate=light(),
        name="feed",
    )(second, hidden, *ups, *downs)
    return out[0], out[1 : 1 + shares], out[1 + shares :]


def ff_back_kernel(shares, per, *refs):
    grad_ref, hidden_ref, gain_ref = refs[:3]
    slope_refs = refs[3 : 3 + shares]
    up_refs, down_refs = refs[3 + shares : 3 + 2 * shares], refs[3 + 2 * shares : 3 + 3 * shares]
    mixed_ref, branch_ref, low_ref, gain_grad_ref = refs[3 + 3 * shares : 7 + 3 * shares]
    inner_refs = refs[7 + 3 * shares :]
    block, chunk = pl.program_id(0), pl.program_id(1)

    @pl.when(chunk == 0)
    def _():
        low_ref[...] = grad_ref[...].astype(jnp.bfloat16)
        mixed_ref[...] = jnp.zeros_like(mixed_ref)

    @pl.when((block == 0) & (chunk == 0))
    def _():
        gain_grad_ref[...] = jnp.zeros_like(gain_grad_ref)

    for share in range(shares):

        @pl.when((chunk >= share * per) & (chunk < (share + 1) * per))
        def _():
            ranges = spans(grad_ref.shape[0], 800)
            up, down = up_refs[share][...], down_refs[share][...]
            ahead = nt(low_ref[ranges[0][0] : ranges[0][1], :], down)
            for at, (start, end) in enumerate(ranges):
                grad_active = ahead
                if at + 1 < len(ranges):
                    ahead = nt(low_ref[ranges[at + 1][0] : ranges[at + 1][1], :], down)
                slope = slope_refs[share][start:end, :].astype(jnp.float32)
                inner = (grad_active * slope).astype(jnp.bfloat16)
                inner_refs[share][start:end, :] = inner
                mixed_ref[start:end, :] += nt(inner, up)

    @pl.when(chunk == shares * per - 1)
    def _():
        def work(rows):
            normal, inverse = standard(hidden_ref[rows, :])
            back, gain_grad = standard_back(mixed_ref[rows, :], normal, inverse, gain_ref[...])
            total = grad_ref[rows, :] + back
            mixed_ref[rows, :] = total
            branch_ref[rows, :] = total.astype(jnp.bfloat16)
            gain_grad_ref[...] += gain_grad

        by_rows(grad_ref.shape[0], work)


def feed_back(grad, hidden, gain, slopes, ups, downs):
    rows, shares = grad.shape[0], len(ups)
    block, width, units, size, per = ff_sizes(rows, ups, 512)
    line = pl.BlockSpec((block, width), lambda at, chunk: (at, 0))
    gain = gain[None]
    piece = [share_spec((block, size), 2, share, per) for share in range(shares)]
    out = pl.pallas_call(
        partial(ff_back_kernel, shares, per),
        grid=(rows // block, shares * per),
        in_specs=[line, line, whole_spec(gain)]
        + piece
        + [share_spec((width, size), 1, share, per) for share in range(shares)]
        + [share_spec((size, width), 0, share, per) for share in range(shares)],
        out_specs=[line, line, line, eight_spec(width)] + piece,
        out_shape=[
            jax.ShapeDtypeStruct((rows, width), jnp.float32),
            jax.ShapeDtypeStruct((rows, width), jnp.bfloat16),
            jax.ShapeDtypeStruct((rows, width), jnp.bfloat16),
            jax.ShapeDtypeStruct((8, width), jnp.float32),
        ]
        + [jax.ShapeDtypeStruct((rows, units), jnp.bfloat16)] * shares,
        compiler_params=params(50),
        cost_estimate=light(),
        name="feed_back",
    )(grad, hidden, gain, *slopes, *ups, *downs)
    return out[0], out[1], out[2], jnp.sum(out[3], axis=0), out[4:]


def split(value):
    high = value.astype(jnp.bfloat16)
    return high, (value - high.astype(jnp.float32)).astype(jnp.bfloat16)


def learn_kernel(bias_ref, input_ref, gain_ref, maps_ref, tokens_ref, shares_ref, high, low_part):
    def work(rows):
        high[rows, :], low_part[rows, :] = split(standard(input_ref[rows, :])[0])

    by_eights(input_ref.shape[0], work)
    maps = jnp.concatenate(split(maps_ref[...] * gain_ref[...]))
    logits = nt(maps, high[...])
    logits = logits[:S] + logits[S:] + nt(maps[:S], low_part[...])
    logits = jnp.concatenate([logits] * (bias_ref.shape[1] // S), axis=0) + bias_ref[0]
    weights = jnp.exp(logits - jnp.max(logits, axis=-1, keepdims=True))
    shares = weights / jnp.sum(weights, axis=-1, keepdims=True)
    shares_ref[0] = shares

    def cut(rows):
        high[rows, :], low_part[rows, :] = split(input_ref[rows, :])

    by_eights(input_ref.shape[0], cut)
    both = jnp.concatenate(split(shares))
    tokens, count = mm(both, high[...]), shares.shape[0]
    tokens_ref[...] = tokens[:count] + tokens[count:] + mm(both[:count], low_part[...])


def by_eights(rows, work):
    for at in range(0, rows, 112):
        work(pl.ds(at, min(112, rows - at)))


def pair_bias(keep):
    step = 4 if keep.shape[0] % 4 == 0 else 2
    seen = keep.reshape(-1, 1, step * P_SIZE)
    own = (jnp.arange(step * S)[:, None] // S) == (jnp.arange(step * P_SIZE)[None] // P_SIZE)
    return jnp.where(seen & own[None], 0.0, -1e30).astype(jnp.float32)


def learn(bias, patched, gain, maps):
    rows, width = patched.shape
    steps, count, span = bias.shape
    gain = gain[None]
    line = pl.BlockSpec((span, width), lambda at: (at, 0))
    mark = pl.BlockSpec((1, count, span), lambda at: (at, 0, 0))
    return pl.pallas_call(
        learn_kernel,
        grid=(steps,),
        in_specs=[mark, line, whole_spec(gain), whole_spec(maps)],
        out_specs=[pl.BlockSpec((count, width), lambda at: (at, 0)), mark],
        out_shape=[
            jax.ShapeDtypeStruct((steps * count, width), jnp.float32),
            jax.ShapeDtypeStruct(bias.shape, jnp.float32),
        ],
        scratch_shapes=[pltpu.VMEM((span, width), jnp.bfloat16)] * 2,
        compiler_params=params(24),
        cost_estimate=light(),
        name="learn",
    )(bias, patched, gain, maps)


def outer(left, right):
    (left_high, left_low), (right_high, right_low) = split(left), split(right)
    return tn(
        jnp.concatenate((left_high, left_high, left_low)),
        jnp.concatenate((right_high, right_low, right_high)),
    )


def learn_back_kernel(
    shares_ref, grad_ref, input_ref, gain_ref, maps_ref,
    out_ref, low_ref, gain_grad_ref, maps_grad_ref, high, low_part, inverses, slope,
):
    @pl.when(pl.program_id(0) == 0)
    def _():
        gain_grad_ref[...] = jnp.zeros_like(gain_grad_ref)
        maps_grad_ref[...] = jnp.zeros_like(maps_grad_ref)

    def cut(rows):
        high[rows, :], low_part[rows, :] = split(input_ref[rows, :])

    by_eights(input_ref.shape[0], cut)
    shares, grad = shares_ref[0], grad_ref[...]
    both = jnp.concatenate(split(grad))
    product, count = nt(both, high[...]), shares.shape[0]
    product = product[:count] + product[count:] + nt(both[:count], low_part[...])
    product = shares * product
    logits = product - shares * jnp.sum(product, axis=-1, keepdims=True)
    logits = sum(logits[at : at + S] for at in range(S, count, S)) + logits[:S]
    slope[...] = outer(logits, maps_ref[...])
    out_ref[...] = outer(shares, grad)

    def before(rows):
        normal, inverse = standard(input_ref[rows, :])
        high[rows, :], low_part[rows, :] = split(normal)
        inverses[rows, :] = jnp.broadcast_to(inverse, inverses[rows, :].shape)

    by_eights(input_ref.shape[0], before)
    both = jnp.concatenate(split(logits))
    maps_grad = mm(both, high[...])
    maps_grad = maps_grad[:S] + maps_grad[S:] + mm(both[:S], low_part[...])
    maps_grad_ref[...] += maps_grad * gain_ref[...]

    def after(rows):
        normal = high[rows, :].astype(jnp.float32) + low_part[rows, :].astype(jnp.float32)
        back, gain_grad = standard_back(
            slope[rows, :], normal, inverses[rows, 0:1], gain_ref[...]
        )
        total = out_ref[rows, :] + back
        out_ref[rows, :] = total
        low_ref[rows, :] = total.astype(jnp.bfloat16)
        gain_grad_ref[...] += gain_grad

    by_eights(input_ref.shape[0], after)


def learn_back(shares, grad, patched, gain, maps):
    rows, width = patched.shape
    steps, count, span = shares.shape
    gain = gain[None]
    line = pl.BlockSpec((span, width), lambda at: (at, 0))
    mark = pl.BlockSpec((1, count, span), lambda at: (at, 0, 0))
    out = pl.pallas_call(
        learn_back_kernel,
        grid=(steps,),
        in_specs=[
            mark,
            pl.BlockSpec((count, width), lambda at: (at, 0)),
            line,
            whole_spec(gain),
            whole_spec(maps),
        ],
        out_specs=[line, line, eight_spec(width), whole_spec(maps)],
        out_shape=[
            jax.ShapeDtypeStruct((rows, width), jnp.float32),
            jax.ShapeDtypeStruct((rows, width), jnp.bfloat16),
            jax.ShapeDtypeStruct((8, width), jnp.float32),
            jax.ShapeDtypeStruct(maps.shape, jnp.float32),
        ],
        scratch_shapes=[
            pltpu.VMEM((span, width), jnp.bfloat16),
            pltpu.VMEM((span, width), jnp.bfloat16),
            pltpu.VMEM((span, 128), jnp.float32),
            pltpu.VMEM((span, width), jnp.float32),
        ],
        compiler_params=params(36),
        cost_estimate=light(),
        name="learn_back",
    )(shares, grad, patched, gain, maps)
    return out[0], out[1], jnp.sum(out[2], axis=0), out[3]


def inward_back_kernel(shares, *refs):
    grad_refs, weight_refs = refs[:shares], refs[shares : 2 * shares]
    later_ref, input_ref, gain_ref, out_ref, gain_grad_ref = refs[2 * shares :]

    @pl.when(pl.program_id(0) == 0)
    def _():
        gain_grad_ref[...] = jnp.zeros_like(gain_grad_ref)

    total = None
    for grad_ref, weight_ref in zip(grad_refs, weight_refs):
        for at in range(3):
            term = nt(grad_ref[at], weight_ref[at])
            total = term if total is None else total + term
    out_ref[...] = total

    def work(rows):
        normal, inverse = standard(input_ref[rows, :])
        back, gain_grad = standard_back(out_ref[rows, :], normal, inverse, gain_ref[...])
        out_ref[rows, :] = later_ref[rows, :] + back
        gain_grad_ref[...] += gain_grad

    by_rows(input_ref.shape[0], work)


def inward_back(grads, weights, later, inputs, gain):
    rows, width = inputs.shape
    block = row_block(rows, 400)
    line = pl.BlockSpec((block, width), lambda at: (at, 0))
    gain = gain[None]
    heads = grads[0].shape[2]
    out = pl.pallas_call(
        partial(inward_back_kernel, len(grads)),
        grid=(rows // block,),
        in_specs=[pl.BlockSpec((3, block, heads), lambda at: (0, at, 0))] * len(grads)
        + [
            pl.BlockSpec((3, width, heads), lambda at, panel=panel: (0, 0, panel))
            for _, panel in weights
        ]
        + [line, line, whole_spec(gain)],
        out_specs=[line, eight_spec(width)],
        out_shape=[
            jax.ShapeDtypeStruct((rows, width), jnp.float32),
            jax.ShapeDtypeStruct((8, width), jnp.float32),
        ],
        compiler_params=params(28),
        cost_estimate=light(),
        name="inward_back",
    )(*grads, *(weight for weight, _ in weights), later, inputs, gain)
    return out[0], jnp.sum(out[1], axis=0)


def few_kernel(shares, *refs):
    input_ref, gain_one_ref, gain_two_ref, bias_ref = refs[:4]
    qkv_refs, out_refs = refs[4 : 4 + shares], refs[4 + shares : 4 + 2 * shares]
    across_ref, hidden_ref, second_ref = refs[4 + 2 * shares : 7 + 2 * shares]
    projected_refs = refs[7 + 2 * shares : 7 + 3 * shares]
    context_refs = refs[7 + 3 * shares :]
    total = input_ref[...]
    across = (standard(total)[0] * gain_one_ref[...]).astype(jnp.bfloat16)
    across_ref[...] = across
    for share in range(shares):
        parts = [mm(across, qkv_refs[share][at]).astype(jnp.bfloat16) for at in range(3)]
        for at, part in enumerate(parts):
            projected_refs[share][at] = part
        for first in range(0, parts[0].shape[1], 2 * HEAD_DIM):
            query, keys, values = (part[:, first : first + 2 * HEAD_DIM] for part in parts)
            context_refs[share][:, first : first + 2 * HEAD_DIM] = mix(
                scaled(query), keys, values, bias_ref[...]
            )
    for share in range(shares):
        total = total + mm(context_refs[share][...], out_refs[share][...])
    hidden_ref[...] = total
    second_ref[...] = (standard(total)[0] * gain_two_ref[...]).astype(jnp.bfloat16)


def few(inputs, gain_one, gain_two, bias, weights_qkv, weights_out):
    rows, width = inputs.shape
    shares, columns = len(weights_qkv), weights_qkv[0].shape[2]
    line = jax.ShapeDtypeStruct((rows, width), jnp.bfloat16)
    out = pl.pallas_call(
        partial(few_kernel, shares),
        out_shape=[line, jax.ShapeDtypeStruct((rows, width), jnp.float32), line]
        + [jax.ShapeDtypeStruct((3, rows, columns), jnp.bfloat16)] * shares
        + [jax.ShapeDtypeStruct((rows, columns), jnp.bfloat16)] * shares,
        compiler_params=params(28),
        cost_estimate=light(),
        name="few",
    )(inputs, gain_one[None], gain_two[None], bias, *weights_qkv, *weights_out)
    return out[0], out[1], out[2], out[3 : 3 + shares], out[3 + shares :]


def few_back_kernel(shares, *refs):
    branch_ref, later_ref, input_ref, gain_ref, bias_ref = refs[:5]
    projected_refs = refs[5 : 5 + shares]
    qkv_refs, out_refs = refs[5 + shares : 5 + 2 * shares], refs[5 + 2 * shares : 5 + 3 * shares]
    grad_ref, gain_grad_ref = refs[5 + 3 * shares : 7 + 3 * shares]
    back_refs = refs[7 + 3 * shares :]
    total = None
    for share in range(shares):
        grad = nt(branch_ref[...], out_refs[share][...]).astype(jnp.bfloat16)
        for first in range(0, grad.shape[1], 2 * HEAD_DIM):
            pair = slice(first, first + 2 * HEAD_DIM)
            query, keys, values = (projected_refs[share][at, :, pair] for at in range(3))
            parts = mix_back(scaled(query), keys, values, grad[:, pair], bias_ref[...])
            for at, part in enumerate(parts):
                back_refs[share][at, :, pair] = part
    for share in range(shares):
        for at in range(3):
            term = nt(back_refs[share][at], qkv_refs[share][at])
            total = term if total is None else total + term
    normal, inverse = standard(input_ref[...])
    back, gain_grad = standard_back(total, normal, inverse, gain_ref[...])
    grad_ref[...] = later_ref[...] + back
    gain_grad_ref[...] = gain_grad


def few_back(branch, later, inputs, gain, bias, projected, weights_qkv, weights_out):
    rows, width = inputs.shape
    shares, columns = len(weights_qkv), weights_qkv[0].shape[2]
    out = pl.pallas_call(
        partial(few_back_kernel, shares),
        out_shape=[
            jax.ShapeDtypeStruct((rows, width), jnp.float32),
            jax.ShapeDtypeStruct((8, width), jnp.float32),
        ]
        + [jax.ShapeDtypeStruct((3, rows, columns), jnp.bfloat16)] * shares,
        compiler_params=params(28),
        cost_estimate=light(),
        name="few_back",
    )(branch, later, inputs, gain[None], bias, *projected, *weights_qkv, *weights_out)
    return out[0], jnp.sum(out[1], axis=0), out[2:]


def again_kernel(rows_refs, up_ref, down_ref, up_grad_ref, down_grad_ref):
    def work(second_ref, grad_ref, begin):
        second, grad = second_ref[...], grad_ref[...]
        up, down = up_ref[...], down_ref[...]
        actives, inners = [], []
        ranges = spans(second.shape[0], 256)
        ahead = mm(second[ranges[0][0] : ranges[0][1]], up)
        for at, (start, end) in enumerate(ranges):
            upward = ahead
            grad_active = nt(grad[start:end], down)
            if at + 1 < len(ranges):
                ahead = mm(second[ranges[at + 1][0] : ranges[at + 1][1]], up)
            active, slope = gelu_pair(upward)
            actives.append(active)
            inners.append((grad_active * slope.astype(jnp.float32)).astype(jnp.bfloat16))
        active, inner = jnp.concatenate(actives), jnp.concatenate(inners)
        if begin:
            down_grad_ref[...] = tn(active, grad)
            up_grad_ref[...] = tn(second, inner)
        else:
            down_grad_ref[...] += tn(active, grad)
            up_grad_ref[...] += tn(second, inner)

    @pl.when(pl.program_id(1) == 0)
    def _():
        work(rows_refs[0], rows_refs[1], True)

    @pl.when(pl.program_id(1) == 1)
    def _():
        work(rows_refs[2], rows_refs[3], False)


def again(piece, pieces, rows, up, down, before):
    width, units = up.shape
    size = min(512, units // pieces)
    first = piece * (units // pieces // size)
    spots = [
        pl.BlockSpec((width, size), lambda chunk, part: (0, first + chunk)),
        pl.BlockSpec((size, width), lambda chunk, part: (first + chunk, 0)),
    ]

    def kernel(*refs):
        again_kernel(refs[:4], *refs[4:6], *refs[-2:])

    return pl.pallas_call(
        kernel,
        grid=(units // pieces // size, 2),
        in_specs=[whole_spec(array) for array in rows]
        + spots
        + [pl.BlockSpec(memory_space=pl.ANY)] * len(before),
        out_specs=spots,
        out_shape=[
            jax.ShapeDtypeStruct(up.shape, jnp.float32),
            jax.ShapeDtypeStruct(down.shape, jnp.float32),
        ],
        input_output_aliases={6: 0, 7: 1} if before else {},
        compiler_params=params(48),
        cost_estimate=light(),
        name="again",
    )(*rows, up, down, *before)


def swap(tensor, bit):
    count = lax.axis_size("dp")
    return lax.ppermute(tensor, "dp", [(place, place ^ (1 << bit)) for place in range(count)])


def my_bit(bit):
    return ((lax.axis_index("dp") >> bit) & 1).astype(jnp.int32).reshape(1)


def meet(value, others):
    if not others:
        return value, []
    value, others = lax.optimization_barrier((value, tuple(others)))
    return value, list(others)


def part_of(number, step, count, mine):
    first = number == mine
    return jnp.where(first, jnp.minimum(step, count - 1), jnp.maximum(step - count, 0))


def divisor(size, most):
    return max(step for step in range(16, most + 1, 16) if size % step == 0)


def fold_kernel(cuts, count, mine_ref, *refs):
    kept_ref, sent_ref = refs[-2:]
    step = pl.program_id(0)
    keep = (step < count) == (mine_ref[0] == 0)
    at = 0
    for first, last, terms in cuts:
        inside = (step >= first) & (step < last)
        sources, at = refs[at : at + terms], at + terms

        def value(sources=sources):
            total = sources[0][...].astype(jnp.float32)
            for source in sources[1:]:
                total = total + source[...].astype(jnp.float32)
            return total.astype(jnp.bfloat16)

        @pl.when(inside & keep)
        def _():
            kept_ref[...] = value()

        @pl.when(inside & jnp.logical_not(keep))
        def _():
            sent_ref[...] = value()


def fold(sources, width, mine):
    total = sum(rows for _, _, rows, _ in sources)
    block = divisor(math.gcd(total // 2, *(value for s in sources for value in s[1:3])), 512)
    count = total // 2 // block
    cuts, specs, terms, at = [], [], [], 0
    for arrays, start, rows, panel in sources:
        steps = rows // block

        def place(step, mine_ref, at=at, steps=steps, start=start // block, panel=panel):
            return start + jnp.clip(step - at, 0, steps - 1), panel

        cuts.append((at, at + steps, len(arrays)))
        specs += [pl.BlockSpec((block, width), place)] * len(arrays)
        terms += arrays
        at += steps
    half = jax.ShapeDtypeStruct((total // 2, width), jnp.bfloat16)
    return pl.pallas_call(
        partial(fold_kernel, cuts, count),
        grid_spec=pltpu.PrefetchScalarGridSpec(
            num_scalar_prefetch=1,
            grid=(2 * count,),
            in_specs=specs,
            out_specs=[
                pl.BlockSpec((block, width), lambda i, m: (part_of(m[0], i, count, 0), 0)),
                pl.BlockSpec((block, width), lambda i, m: (part_of(1 - m[0], i, count, 0), 0)),
            ],
        ),
        out_shape=[half, half],
        compiler_params=params(18),
        cost_estimate=light(),
        name="fold",
    )(mine, *terms)


def put(out_ref, value):
    value = value.astype(out_ref.dtype)
    if len(out_ref.shape) == 2:
        out_ref[...] = value
        return
    wide = out_ref.shape[2]
    for at in range(3):
        out_ref[at] = value[:, at * wide : (at + 1) * wide]


def spread_kernel(cuts, parts, mines_ref, *refs):
    outs = refs[2 * len(parts) :]
    step = pl.program_id(0)
    for at, (begin, count) in enumerate(parts):
        own_ref, got_ref = refs[2 * at : 2 * at + 2]
        own = (step < begin + count) == (mines_ref[at] == 0)
        for first, last, out in cuts[at]:
            inside = (step >= first) & (step < last)

            @pl.when(inside & own)
            def _():
                put(outs[out], own_ref[...])

            @pl.when(inside & jnp.logical_not(own))
            def _():
                put(outs[out], got_ref[...])


def spread(pieces, layouts, outs, dtype):
    width = pieces[0][0].shape[1]
    sizes = [piece[0].shape[0] for piece in pieces]
    sizes += [value for layout in layouts for entry in layout for value in entry[1:3]]
    block = divisor(math.gcd(*sizes), 512)
    parts, cuts, specs, terms, step = [], [], [], [], 0
    visits = [[] for _ in outs]
    for at, (own, got, _) in enumerate(pieces):
        count = own.shape[0] // block
        parts.append((step, count))
        for half in range(2):

            def place(i, m, at=at, half=half, begin=step, count=count):
                i = jnp.clip(i - begin, 0, 2 * count - 1)
                return part_of(m[at] if half == 0 else 1 - m[at], i, count, 0), 0

            specs.append(pl.BlockSpec((block, width), place))
        terms += [own, got]
        mine, first = [], step
        for out, start, rows, panel in layouts[at]:
            steps = rows // block
            mine.append((first, first + steps, out))
            visits[out].append((first, steps, start // block, panel))
            first += steps
        cuts.append(mine)
        step += 2 * count

    def out_spec(seen, shape):
        def place(i, m):
            row, panel = seen[0][2], seen[0][3]
            for first, steps, start, column in seen:
                here = i >= first
                row = jnp.where(here, start + jnp.clip(i - first, 0, steps - 1), row)
                panel = jnp.where(here, column, panel)
            return (row, panel) if len(shape) == 2 else (0, row, panel)

        if len(shape) == 3:
            return pl.BlockSpec((3, block, width // 3), place)
        return pl.BlockSpec((block, width), place)

    return pl.pallas_call(
        partial(spread_kernel, cuts, parts),
        grid_spec=pltpu.PrefetchScalarGridSpec(
            num_scalar_prefetch=1,
            grid=(step,),
            in_specs=specs,
            out_specs=[out_spec(seen, shape) for seen, shape in zip(visits, outs)],
        ),
        out_shape=[jax.ShapeDtypeStruct(shape, dtype) for shape in outs],
        compiler_params=params(22),
        cost_estimate=light(),
        name="spread",
    )(jnp.concatenate([mine for _, _, mine in pieces]), *terms)


def join(own, got, mine):
    rows, width = own.shape
    layout = [(0, 0, 2 * rows, 0)]
    return spread([(own, got, mine)], [layout], [(2 * rows, width)], own.dtype)[0]


class Flow:
    def __init__(self, halves, order, back=False):
        self.order, self.step = order, 0
        self.kept, self.sent = halves
        self.got = swap(self.sent, order[0])
        self.length = 2 * len(order) - 1 if back else len(order)

    def done(self):
        return self.step == self.length

    def advance(self):
        self.step += 1
        bits, turn = self.order, len(self.order)
        if self.step < turn:
            rows, width = self.kept.shape
            bit = bits[self.step]
            self.kept, self.sent = fold([((self.kept, self.got), 0, rows, 0)], width, my_bit(bit))
        elif self.step == turn:
            bit = bits[-1]
            total = self.kept.astype(jnp.float32) + self.got.astype(jnp.float32)
            self.kept = self.sent = total.astype(jnp.bfloat16)
        else:
            bit = bits[2 * turn - 1 - self.step]
            self.kept = self.sent = join(self.kept, self.got, my_bit(bits[2 * turn - self.step]))
        if self.step < self.length or self.length > turn:
            self.got = swap(self.sent, bit)


def in_order(gathered, order):
    count = len(order)
    rows, width = gathered.shape[1:]
    split = gathered.reshape((2,) * count + (rows, width))
    axes = tuple(count - 1 - bit for bit in order) + (count, count + 1)
    return jnp.transpose(split, axes).reshape(-1, width)


class Gather:
    def __init__(self, rows):
        self.step, self.length = 0, lax.axis_size("dp").bit_length()
        self.kept = self.sent = rows
        self.got = swap(rows, 0)

    def done(self):
        return self.step == self.length

    def advance(self):
        self.step += 1
        if self.step < self.length:
            self.kept = self.sent = join(self.kept, self.got, my_bit(self.step - 1))
            last = self.step == self.length - 1
            self.got = near(1)(self.kept) if last else swap(self.kept, self.step)


class Small:
    def __init__(self, tensors):
        self.kept = self.sent = jnp.concatenate(tensors)
        self.step, self.length = 0, lax.axis_size("mp") - 1
        self.length += lax.axis_size("dp").bit_length() - 1
        self.mine = self.kept
        self.issue()

    def issue(self):
        near_by = lax.axis_size("mp") - 1
        if self.step < near_by:
            self.got = give(self.step + 1)(self.mine)
        else:
            self.got = swap(self.kept, self.step - near_by)

    def done(self):
        return self.step == self.length

    def advance(self):
        self.kept = self.sent = self.kept + self.got
        self.step += 1
        if not self.done():
            self.issue()


class Clock:
    def __init__(self, plan, sets):
        self.plan, self.sets = plan, dict(sets)
        self.flows, self.begun, self.past, self.whole = {}, [], [], {}

    def begin(self, name, flow):
        self.flows[name] = flow
        self.begun.append(flow.sent)

    def __call__(self, name, value):
        names = self.plan.get(name, ())
        flows = [self.flows[flow] for flow in names if flow in self.flows]
        ended = [flow for flow in flows if flow.done()]
        flows = [flow for flow in flows if not flow.done()]
        ready = [key for key in names if key in self.whole]
        waited = [flow.got for flow in flows] + [self.whole[key] for key in ready]
        waited += [flow.got for flow in ended]
        value, got = meet(value, waited + self.past)
        self.past = []
        for flow in flows:
            flow.got = got.pop(0)
            flow.advance()
        for key in ready:
            self.whole[key] = got.pop(0)
        for flow in ended:
            flow.got = got.pop(0)
        for key, members in list(self.sets.items()):
            if all(name in self.flows and self.flows[name].done() for name in members):
                self.begun.append(self.gather(key))
        value = meet(value, self.begun + [flow.sent for flow in flows])[0]
        self.begun = []
        return value

    def gather(self, key):
        kept = [self.flows[name].kept for name in self.sets.pop(key)]
        own = jnp.concatenate(kept) if len(kept) > 1 else kept[0]
        self.whole[key] = lax.all_gather(own, "dp")
        return own

    def end(self, names):
        flows = [self.flows[name] for name in names]
        while not all(flow.done() for flow in flows):
            for flow in flows:
                if not flow.done():
                    flow.advance()

    def rows(self, names, whole):
        pieces, at = [], 0
        for flow in (self.flows[name] for name in names):
            own = flow.kept.shape[0]
            pieces.append(in_order(whole[:, at : at + own], flow.order))
            at += own
        return pieces


def grads_kernel(cuts, count, *refs):
    outs = refs[-2:] if count else refs[-1:]
    step = pl.program_id(0)
    keep = True if not count else (step < count) == (refs[0][0] == 0)
    at = 1
    for first, last, terms in cuts:
        inside = (step >= first) & (step < last)
        sources, at = refs[at : at + terms], at + terms

        @pl.when(inside)
        def _(sources=sources):
            if len(sources[1].shape) == 2:
                total = tn(sources[0][...], sources[1][...])
            else:
                left = sources[0][...].T
                total = jnp.concatenate([mm(left, sources[1][part]) for part in range(3)], axis=1)
            if len(sources) > 2:
                total = total + sources[2][...].astype(jnp.float32)
            total = total.astype(jnp.bfloat16)
            if not count:
                outs[0][...] = total
                return

            @pl.when(keep)
            def _():
                outs[0][...] = total

            @pl.when(jnp.logical_not(keep))
            def _():
                outs[1][...] = total


def grads(sources, width, mine=None):
    total = sum(source[2] for source in sources)
    sizes = [value for source in sources for value in source[1:3]]
    if mine is not None:
        sizes.append(total // 2)
    sizes += [source[6] for source in sources if len(source) > 5]
    block = divisor(math.gcd(*sizes), 512)
    cuts, specs, terms, at = [], [], [], 0
    for source in sources:
        left, start, columns, right, panel = source[:5]
        steps = columns // block
        rows = left.shape[0]

        def here(step, at=at, steps=steps):
            return jnp.clip(step - at, 0, steps - 1)

        specs.append(
            pl.BlockSpec((rows, block), lambda i, *m, f=here, s=start // block: (0, s + f(i)))
        )
        if right.ndim == 2:
            specs.append(pl.BlockSpec((rows, width), lambda i, *m, p=panel: (0, p)))
        else:
            specs.append(whole_spec(right))
        terms += [left, right]
        if len(source) > 5:
            other, row, column = source[5:]
            specs.append(
                pl.BlockSpec(
                    (block, width), lambda i, *m, f=here, s=row // block, p=column: (s + f(i), p)
                )
            )
            terms.append(other)
        cuts.append((at, at + steps, 3 if len(source) > 5 else 2))
        at += steps
    count = 0 if mine is None else total // 2 // block
    if count:
        shape = jax.ShapeDtypeStruct((total // 2, width), jnp.bfloat16)
        out_shape = [shape, shape]
        out_specs = [
            pl.BlockSpec((block, width), lambda i, m: (part_of(m[0], i, count, 0), 0)),
            pl.BlockSpec((block, width), lambda i, m: (part_of(1 - m[0], i, count, 0), 0)),
        ]
    else:
        mine = jnp.zeros((1,), jnp.int32)
        out_shape = jax.ShapeDtypeStruct((total, width), jnp.bfloat16)
        out_specs = pl.BlockSpec((block, width), lambda i, m: (i, 0))
    return pl.pallas_call(
        partial(grads_kernel, cuts, count),
        grid_spec=pltpu.PrefetchScalarGridSpec(
            num_scalar_prefetch=1, grid=(at,), in_specs=specs, out_specs=out_specs
        ),
        out_shape=out_shape,
        compiler_params=params(38),
        cost_estimate=light(),
        name="grads",
    )(mine, *terms)


def near(step):
    count = lax.axis_size("mp")
    pairs = [((to + step) % count, to) for to in range(count)]
    return lambda tensor: lax.ppermute(tensor, "mp", pairs)


def give(step):
    count = lax.axis_size("mp")
    pairs = [(start, (start + step) % count) for start in range(count)]
    return lambda tensor: lax.ppermute(tensor, "mp", pairs)


def fetch(tensor):
    return [tensor] + [near(step)(tensor) for step in range(1, lax.axis_size("mp"))]


def total_over_all(terms):
    total = terms[0].astype(jnp.float32)
    for step in range(1, len(terms)):
        total = total + give(step)(terms[step]).astype(jnp.float32)
    return lax.psum(total.astype(jnp.bfloat16), "dp").astype(jnp.float32)


def lower_forward(inputs, weights, bias, later):
    gain_one, weight_qkv, weight_out, gain_two, weight_up, weight_down = weights
    across = norm(inputs, gain_one)
    projections, contexts = [], []
    for share in weight_qkv:
        projected = jnp.einsum(
            "rd,tdc->trc", across, share, preferred_element_type=jnp.float32
        ).astype(jnp.bfloat16)
        projections.append(projected)
        contexts.append(attend(bias, projected))
    hidden, second = outward(contexts, weight_out, inputs, gain_two)
    second, later = meet(second, later)
    result, actives, slopes = feed(second, hidden, weight_up, weight_down)
    stored = (inputs, hidden, across, second, projections, contexts, actives, slopes)
    return result, stored, later


def upper_forward(inputs, weights, bias, clock):
    gain_one, weight_qkv, weight_out, gain_two, weight_up, weight_down = weights
    across, hidden, second, projections, contexts = few(
        inputs, gain_one, gain_two, bias, weight_qkv, weight_out
    )
    if len(weight_qkv) == 2 and lax.axis_size("dp") == 16:
        clock.begin("seconds", Gather(second))
    second = clock("second-feed", second)
    result, actives, slopes = feed(second, hidden, weight_up, weight_down)
    return result, (inputs, hidden, across, second, projections, contexts, actives, slopes)


def low(value):
    return value.astype(jnp.bfloat16)


def project_sources(across, back, others=None):
    source = (across, 0, across.shape[1], back, 0)
    return [source if others is None else source + (others, 0, 0)]


def out_sources(context, grad_branch, wide, others=None, first=0):
    rows = context.shape[1]
    panels = range(grad_branch.shape[1] // wide)
    sources = [(context, 0, rows, grad_branch, panel) for panel in panels]
    if others is None:
        return sources
    return [source + (others, first + at * rows, 0) for at, source in enumerate(sources)]


def upper_backward(grad_out, stored, weights, bias, clock):
    gain_one, weight_qkv, weight_out, gain_two, weight_up, weight_down = weights
    inputs, hidden, across, second, projections, contexts, actives, slopes = stored
    shares = range(len(weight_qkv))
    grad_out = clock("second-back", grad_out)
    grad_hidden, grad_branch, grad_mix, grad_gain_two, inners = feed_back(
        grad_out, hidden, gain_two, slopes, weight_up, weight_down
    )
    quick = len(shares) == 2 and lax.axis_size("dp") == 16
    grad_branch = clock("second-few", grad_branch)
    grad_inputs, grad_gain_one, backs = few_back(
        grad_branch, grad_hidden, inputs, gain_one, bias, projections, weight_qkv, weight_out
    )
    if quick:
        projects = grads(project_sources(across, backs[1]), 3 * contexts[0].shape[1])
        clock.past.append(projects)
        weight_grads = (across, backs, contexts, grad_branch, give(1)(projects))
    else:
        weight_grads = plain_grads(
            across, backs, contexts, grad_branch, second, inners, actives, grad_mix
        )
    return grad_inputs, grad_gain_one, grad_gain_two, weight_grads


def plain_grads(across, backs, contexts, grad_branch, second, inners, actives, grad_mix):
    shares = range(len(contexts))
    pairs = (
        [jnp.concatenate([tn(across, part) for part in backs[at]]) for at in shares],
        [tn(contexts[at], grad_branch) for at in shares],
        [tn(second, inners[at]) for at in shares],
        [tn(actives[at], grad_mix) for at in shares],
    )
    return tuple(total_over_all([low(term) for term in terms]) for terms in pairs)


def lower_backward(grad_out, grad_mix, stored, weights, bias, clock, upper_sources):
    gain_one, weight_qkv, weight_out, gain_two, weight_up, weight_down = weights
    inputs, hidden, across, second, projections, contexts, actives, slopes = stored
    shares = range(len(weight_qkv))
    quick = len(shares) == 2 and lax.axis_size("dp") == 16
    bits = tuple(range(lax.axis_size("dp").bit_length() - 1))
    turned = (1, 0) + bits[2:]
    width, units = weight_up[0].shape
    wide = contexts[0].shape[1]
    if quick:
        upper_across, upper_backs, upper_contexts, upper_branch, project_others = upper_sources
        grad_mix, (project_others,) = meet(clock("down1", grad_mix), [project_others])
        heads = 3 * wide
        sources = [(actives[1], 0, units, grad_mix, 0)]
        others = grads(sources + out_sources(upper_contexts[1], upper_branch, width), width)
        upper_across = meet(upper_across, [others])[0]
        others = give(1)(others)
        sources = project_sources(upper_across, upper_backs[0], project_others)
        halves = grads(sources, heads, my_bit(bits[0]))
        clock.begin("heads", Flow(halves, bits, True))
        grad_mix = meet(grad_mix, halves)[0]
        sources = [(actives[0], 0, units, grad_mix, 0, others, 0, 0)]
        sources += out_sources(upper_contexts[0], upper_branch, width, others, units)
        clock.begin("down", Flow(grads(sources, width, my_bit(turned[0])), turned, True))
    grad_out = clock("feed", grad_out)
    grad_hidden, grad_branch, grad_mix, grad_gain_two, inners = feed_back(
        grad_out, hidden, gain_two, slopes, weight_up, weight_down
    )
    if quick:
        panels = range(units // width)
        grad_branch = clock("up1", grad_branch)
        sources = [(second, 0, width, inners[1], panel) for panel in panels]
        sources += out_sources(contexts[1], grad_branch, width)
        up_others = grads(sources, width)
        grad_branch = meet(grad_branch, [up_others])[0]
        up_others = give(1)(up_others)
    groups = 2 if quick and wide % (4 * HEAD_DIM) == 0 else 1
    backs, grad_contexts = {}, {}
    for group in range(groups):
        for at in reversed(shares):
            if group == 0:
                grad_branch = clock(f"heads{group}{at}", grad_branch)
                grad_contexts[at] = low(nt(grad_branch, weight_out[at]))
            else:
                grad_contexts[at] = clock(f"heads{group}{at}", grad_contexts[at])
            back = attend_back(bias, projections[at], grad_contexts[at], group, groups)
            backs[at, group] = back = clock(f"project{group}{at}", back)
            if quick and at:
                others = grads(project_sources(across, back), 3 * wide // groups)
                clock.past.append(others)
                others = give(at)(others)
            elif quick:
                sources = project_sources(across, back, others)
                order = turned if group else bits
                halves = grads(sources, 3 * wide // groups, my_bit(order[0]))
                clock.past += halves
                clock.begin(f"project-{group}", Flow(halves, order, True))
            if quick and at and group == 0:
                grad_branch = clock("up0", grad_branch)
                for panel in panels:
                    sources = [
                        (second, 0, width, inners[0], panel, up_others, panel * width, 0)
                    ]
                    if panel == len(panels) - 1:
                        sources += out_sources(contexts[0], grad_branch, width, up_others, units)
                    sources[0] = (meet(second, [grad_branch])[0],) + sources[0][1:]
                    order = turned if panel % 2 else bits
                    halves = grads(sources, width, my_bit(order[0]))
                    clock.past += halves
                    clock.begin(f"up-{panel}", Flow(halves, order))
    weight_grads = None
    if not quick:
        whole_backs = [backs[at, 0] for at in shares]
        weight_grads = plain_grads(
            across, whole_backs, contexts, grad_branch, second, inners, actives, grad_mix
        )
    inputs = clock("inward", inputs)
    grad_inputs, grad_gain_one = inward_back(
        [backs[at, group] for at in shares for group in range(groups)],
        [(weight_qkv[at], group) for at in shares for group in range(groups)],
        grad_hidden,
        inputs,
        gain_one,
    )
    return grad_inputs, grad_gain_one, grad_gain_two, weight_grads


PLAN = {
    "learn": ("mixes",),
    "second-back": ("seconds",),
    "second-few": ("seconds",),
    "learner": ("seconds",),
    "up1": ("heads", "down", "seconds"),
    "heads00": ("heads", "down", "seconds"),
    "heads11": ("heads", "down", "up-0", "up-1"),
    "project11": ("up-0", "up-1", "project-0"),
    "heads10": ("heads", "down", "up-0", "up-1"),
    "project10": ("up-0", "up-1", "project-0"),
    "inward": ("heads", "down", "project-0"),
    "tail0": ("heads", "down", "project-0", "project-1"),
    "tail1": ("project-0", "project-1", "small"),
    "tail2": ("project-0", "project-1", "small"),
    "tail3": ("project-0", "project-1", "small", "up-all"),
    "tail4": ("project-1", "small"),
    "again0": ("heads", "down", "project-1", "small"),
    "again1": ("project-1",),
    "tail5": ("heads", "down", "project-1"),
}
SETS = {"up-all": ("up-0", "up-1")}


def finish(clock, input_grad, project, out, up, down, token_up, token_down):
    width, wide, units = project.shape[1], project.shape[2], up.shape[1]
    wider = jnp.float32
    ups = [f"up-{panel}" for panel in range(units // width)]
    seconds, mixes = clock.flows["seconds"], clock.whole["mixes"]
    rows = [seconds.kept, mixes, seconds.got, near(1)(mixes)]
    rows[0] = meet(rows[0], [input_grad])[0]
    for number in range(4):
        rows[0] = clock(f"tail{number}", rows[0])
    panels = clock.rows(ups, clock.whole["up-all"])
    panels, out_grad = panels[:-1] + [panels[-1][:width]], panels[-1][width:]
    patch_upward_grad = jnp.concatenate(panels, axis=1).astype(wider)
    rows[0], late = meet(rows[0], [patch_upward_grad, out_grad])
    patch_upward_grad, out_grad = late
    rows[0] = clock("tail4", rows[0])
    before = ()
    for piece in range(2):
        rows[0] = clock(f"again{piece}", rows[0])
        before = again(piece, 2, rows, token_up, token_down, before)
        rows[0], before = meet(rows[0], before)
    token_upward_grad, token_downward_grad = before
    token_downward_grad = clock("tail5", token_downward_grad)
    clock.end(clock.flows)

    def last(name):
        flow = clock.flows[name]
        return flow.kept, flow.got, my_bit(flow.order[0])

    patch_downward_grad, token_outproj_grad = spread(
        [last("down")], [[(0, 0, units, 0), (1, 0, wide, 0)]], [down.shape, out.shape], wider
    )
    (token_project_grad,) = spread([last("heads")], [[(0, 0, width, 0)]], [project.shape], wider)
    (patch_project_grad,) = spread(
        [last("project-0"), last("project-1")],
        [[(0, 0, width, 0)], [(0, 0, width, 1)]],
        [project.shape],
        wider,
    )
    return (
        (token_project_grad, token_outproj_grad, token_upward_grad, token_downward_grad),
        (patch_project_grad, out_grad.astype(wider), patch_upward_grad, patch_downward_grad),
    )


def local(
    inputs,
    patch_keep,
    patch_gainone,
    patch_project,
    patch_outproj,
    patch_gaintwo,
    patch_upward,
    patch_downward,
    learner_gain,
    learner_weight,
    token_gainone,
    token_project,
    token_outproj,
    token_gaintwo,
    token_upward,
    token_downward,
    output_grad,
):
    shards = lax.axis_size("mp")
    images_here = patch_keep.shape[0] // shards
    local_keep = (
        lax.dynamic_slice_in_dim(patch_keep, lax.axis_index("mp") * images_here, images_here, 0) > 0
    )
    lower_params = (
        patch_gainone,
        fetch(patch_project),
        fetch(patch_outproj),
        patch_gaintwo,
        fetch(patch_upward),
        fetch(patch_downward),
    )
    lower_bias = key_bias(local_keep)
    image = jnp.arange(images_here * S) // S
    upper_bias = jnp.where(image[:, None] == image[None], 0.0, -1e30).astype(jnp.float32)
    token_weights = [token_project, token_outproj, token_upward, token_downward]
    patched, lower_stored, token_weights = lower_forward(
        inputs, lower_params, lower_bias, token_weights
    )
    weight_qkv, weight_out, weight_up, weight_down = (fetch(weight) for weight in token_weights)
    upper_params = (token_gainone, weight_qkv, weight_out, token_gaintwo, weight_up, weight_down)
    maps = learner_weight.T
    clock = Clock(PLAN, SETS)
    if shards == 2 and lax.axis_size("dp") == 16:
        clock.whole["mixes"] = lax.all_gather(low(output_grad), "dp", tiled=True)
    patched = clock("learn", patched)
    tokens, shares = learn(pair_bias(local_keep), patched, learner_gain, maps)
    token_output, upper_stored = upper_forward(tokens, upper_params, upper_bias, clock)
    token_grad, token_gainone_grad, token_gaintwo_grad, token_grads = upper_backward(
        output_grad, upper_stored, upper_params, upper_bias, clock
    )
    patched_grad, patched_low, learner_gain_grad, maps_grad = learn_back(
        shares, clock("learner", token_grad), patched, learner_gain, maps
    )
    input_grad, patch_gainone_grad, patch_gaintwo_grad, patch_grads = lower_backward(
        patched_grad, patched_low, lower_stored, lower_params, lower_bias, clock, token_grads
    )
    gains = (
        patch_gainone_grad,
        patch_gaintwo_grad,
        learner_gain_grad,
        token_gainone_grad,
        token_gaintwo_grad,
    )
    clock.begin("small", Small([maps_grad] + [gain[None] for gain in gains]))
    if patch_grads is None:
        token_grads, patch_grads = finish(
            clock,
            input_grad,
            patch_project,
            patch_outproj,
            patch_upward,
            patch_downward,
            token_upward,
            token_downward,
        )
    else:
        clock.end(["small"])
    small = clock.flows["small"].kept
    token_project_grad, token_outproj_grad, token_upward_grad, token_downward_grad = token_grads
    patch_project_grad, patch_outproj_grad, patch_upward_grad, patch_downward_grad = patch_grads
    return (
        token_output,
        input_grad,
        small[8],
        patch_project_grad.reshape(patch_project.shape),
        patch_outproj_grad,
        small[9],
        patch_upward_grad,
        patch_downward_grad,
        small[10],
        small[:S].T,
        small[11],
        token_project_grad.reshape(token_project.shape),
        token_outproj_grad,
        small[12],
        token_upward_grad,
        token_downward_grad,
    )


def solution(mesh):
    in_specs = (
        P(("dp", "mp"), None),
        P("dp", None),
        P(),
        P(None, None, "mp"),
        P("mp", None),
        P(),
        P(None, "mp"),
        P("mp", None),
        P(),
        P(),
        P(),
        P(None, None, "mp"),
        P("mp", None),
        P(),
        P(None, "mp"),
        P("mp", None),
        P(("dp", "mp"), None),
    )
    out_specs = (
        P(("dp", "mp"), None),
        P(("dp", "mp"), None),
        P(),
        P(None, None, "mp"),
        P("mp", None),
        P(),
        P(None, "mp"),
        P("mp", None),
        P(),
        P(),
        P(),
        P(None, None, "mp"),
        P("mp", None),
        P(),
        P(None, "mp"),
        P("mp", None),
    )
    return jax.shard_map(local, mesh=mesh, in_specs=in_specs, out_specs=out_specs, check_vma=False)
```

```python
import math
from functools import partial

import jax
import jax.numpy as jnp
from jax import lax
from jax.experimental import pallas as pl
from jax.experimental.pallas import tpu as pltpu
from jax.sharding import PartitionSpec as P

HEAD_DIM = 64
P_SIZE = 196
S = 8


epsilon = 1e-06
highest = lax.Precision.HIGHEST


WINDOW = 208


def key_bias(keep):
    pieces = []
    for place in range(keep.shape[0]):
        offset = place * P_SIZE % 16
        row = jnp.where(keep[place], 0.0, -1e30).astype(jnp.float32)
        pieces.append(jnp.pad(row, (offset, WINDOW - P_SIZE - offset), constant_values=-1e30))
    return jnp.stack(pieces)[:, :, None]


def nt(left, right):
    return lax.dot_general(
        left, right, (((1,), (1,)), ((), ())), preferred_element_type=jnp.float32
    )


def mm(left, right):
    return jnp.dot(left, right, preferred_element_type=jnp.float32)


def only(head, tensor):
    lane = lax.broadcasted_iota(jnp.int32, tensor.shape, 1)
    return jnp.where((lane < HEAD_DIM) == (head == 0), tensor, jnp.zeros_like(tensor))


def pick(pair):
    lane = lax.broadcasted_iota(jnp.int32, pair[0].shape, 1)
    return jnp.where(lane < HEAD_DIM, pair[0], pair[1])


def mix(query, keys, values, bias):
    turned = values.T
    pieces = []
    for head in range(2):
        scores = nt(only(head, keys), query) + bias
        weights = jnp.exp(scores - jnp.max(scores, axis=0, keepdims=True))
        total = jnp.sum(weights, axis=0, keepdims=True)
        mixed = mm(turned[head * HEAD_DIM : (head + 1) * HEAD_DIM], weights.astype(jnp.bfloat16))
        pieces.append(mixed * (1.0 / total))
    return jnp.concatenate(pieces, axis=0).T.astype(jnp.bfloat16)


def mix_back(query, keys, values, grad, bias):
    turned = keys.T
    by_query, by_key, by_value = [], [], []
    for head in range(2):
        scores = nt(only(head, keys), query) + bias
        weights = jnp.exp(scores - jnp.max(scores, axis=0, keepdims=True))
        total = jnp.sum(weights, axis=0, keepdims=True)
        shares = weights * (1.0 / total)
        product = shares * nt(only(head, values), grad)
        inner = jnp.sum(product, axis=0, keepdims=True)
        grad_scores = (product - shares * inner).astype(jnp.bfloat16)
        by_value.append(mm(shares.astype(jnp.bfloat16), grad))
        by_key.append(mm(grad_scores, query))
        by_query.append(mm(turned[head * HEAD_DIM : (head + 1) * HEAD_DIM], grad_scores))
    grad_query = jnp.concatenate(by_query, axis=0).T * HEAD_DIM**-0.5
    return tuple(value.astype(jnp.bfloat16) for value in (grad_query, pick(by_key), pick(by_value)))


def scaled(query):
    return query * jnp.bfloat16(HEAD_DIM**-0.5)


def window_of(place):
    first = place * P_SIZE
    start = first // 16 * 16
    row = lax.broadcasted_iota(jnp.int32, (WINDOW, 2 * HEAD_DIM), 0)
    offset = first - start
    return pl.ds(start, WINDOW), (row >= offset) & (row < offset + P_SIZE)


def attend_kernel(images, bias_ref, qkv_ref, out_ref):
    for place in range(images):
        window, inside = window_of(place)
        mixed = mix(
            scaled(qkv_ref[0, window, :]),
            qkv_ref[1, window, :],
            qkv_ref[2, window, :],
            bias_ref[place],
        )
        out_ref[window, :] = jnp.where(inside, mixed, out_ref[window, :])


def attend_back_kernel(images, bias_ref, qkv_ref, grad_ref, out_ref):
    for place in range(images):
        window, inside = window_of(place)
        grad = grad_ref[window, :]
        parts = mix_back(
            scaled(qkv_ref[0, window, :]),
            qkv_ref[1, window, :],
            qkv_ref[2, window, :],
            jnp.where(inside, grad, jnp.zeros_like(grad)),
            bias_ref[place],
        )
        for at, value in enumerate(parts):
            out_ref[at, window, :] = jnp.where(inside, value, out_ref[at, window, :])


def attention(kernel, bias, projected, grads, panel, panels):
    rows, columns = projected.shape[1:]
    spare = -rows % 16
    if spare:
        projected = jnp.pad(projected, ((0, 0), (0, spare), (0, 0)))
        grads = [jnp.pad(grad, ((0, spare), (0, 0))) for grad in grads]
    wide, columns = 2 * HEAD_DIM, columns // panels
    pairs = columns // wide
    first = panel * pairs
    rows += spare
    plane = pl.BlockSpec((rows, wide), lambda pair: (0, pair))
    triple = pl.BlockSpec((3, rows, wide), lambda pair: (0, 0, pair))
    shape = (rows, columns)
    out = pl.pallas_call(
        kernel,
        grid=(pairs,),
        in_specs=[
            pl.BlockSpec(bias.shape, lambda pair: (0,) * bias.ndim),
            pl.BlockSpec((3, rows, wide), lambda pair: (0, 0, first + pair)),
        ]
        + [pl.BlockSpec((rows, wide), lambda pair: (0, first + pair))] * len(grads),
        out_specs=triple if grads else plane,
        out_shape=jax.ShapeDtypeStruct((3,) + shape if grads else shape, jnp.bfloat16),
        compiler_params=params(14),
        cost_estimate=light() if grads else cost(16 * rows * 1024 * columns, 8 * rows * columns),
        name="attend_back" if grads else "attend",
    )(bias, projected, *grads)
    return out[..., : rows - spare, :] if spare else out


def attend(bias, projected):
    return attention(partial(attend_kernel, bias.shape[0]), bias, projected, [], 0, 1)


def attend_back(bias, projected, grad_context, panel, panels):
    kernel = partial(attend_back_kernel, bias.shape[0])
    return attention(kernel, bias, projected, [grad_context], panel, panels)


def tn(left, right):
    return lax.dot_general(
        left, right, (((0,), (0,)), ((), ())), preferred_element_type=jnp.float32
    )


def row_mean(matrix):
    width = matrix.shape[1]
    folded = matrix[:, :128]
    for at in range(128, width, 128):
        folded = folded + matrix[:, at : at + 128]
    return jnp.sum(folded, axis=-1, keepdims=True) * (1.0 / width)


def standard(matrix):
    center = matrix - row_mean(matrix)
    spread = row_mean(center * center)
    inverse = lax.rsqrt(spread + epsilon)
    return center * inverse, inverse


def standard_back(grad, normal, inverse, gain):
    scaled_grad = grad * gain
    mean = row_mean(scaled_grad)
    along = row_mean(scaled_grad * normal)
    return (
        inverse * (scaled_grad - mean - normal * along),
        jnp.sum((grad * normal).reshape(-1, 8, grad.shape[1]), axis=0),
    )


def gelu_pair(upward):
    bell = jnp.exp(upward * upward * -0.5)
    base = 1.0 + jnp.abs(upward) * (0.3275911 * 0.5**0.5)
    ratio = pl.reciprocal(base, approx=True)
    ratio = ratio * (2.0 - base * ratio)
    series = 0.5 * 1.061405429
    for factor in (-1.453152027, 1.421413741, -0.284496736, 0.254829592):
        series = series * ratio + 0.5 * factor
    tail = series * ratio * bell
    below = jnp.where(upward < 0.0, tail, 1.0 - tail)
    slope = below + upward * bell * (0.5 / math.pi) ** 0.5
    return (upward * below).astype(jnp.bfloat16), slope.astype(jnp.bfloat16)


def spans(rows, most):
    if rows <= most or rows % 16:
        return [(0, rows)]
    parts = -(-rows // most)
    cuts = [rows // 16 * at // parts * 16 for at in range(parts + 1)]
    return list(zip(cuts, cuts[1:]))


def row_block(rows, most):
    for count in range(1, rows + 1):
        if rows % count == 0 and rows // count <= most and rows // count % 16 == 0:
            return rows // count
    return rows


def by_rows(rows, work, step=112):
    size = row_block(rows, 128)

    def run(first):
        for at in range(0, size, step):
            start = first + at
            if not isinstance(start, int):
                start = pl.multiple_of(start, 16)
            work(pl.ds(start, min(step, size - at)))

    if size == rows:
        run(0)
        return

    def one(at, carry):
        run(at * size)
        return carry

    lax.fori_loop(0, rows // size, one, 0)


def light():
    return pl.CostEstimate(flops=1000, bytes_accessed=1000, transcendentals=0)


def cost(flops, moved):
    return pl.CostEstimate(flops=int(flops), bytes_accessed=int(moved), transcendentals=0)


def params(mebibytes):
    return pltpu.CompilerParams(vmem_limit_bytes=mebibytes * 1024 * 1024)


def eight_spec(width):
    return pl.BlockSpec((8, width), lambda *at: (0, 0))


def whole_spec(array):
    return pl.BlockSpec(array.shape, lambda *at: (0,) * array.ndim)


def norm_kernel(input_ref, gain_ref, out_ref):
    def work(rows):
        normal = standard(input_ref[rows, :])[0]
        out_ref[rows, :] = (normal * gain_ref[...]).astype(jnp.bfloat16)

    by_rows(input_ref.shape[0], work)


def norm(inputs, gain):
    rows, width = inputs.shape
    block = row_block(rows, 400)
    line = pl.BlockSpec((block, width), lambda at: (at, 0))
    gain = gain[None]
    return pl.pallas_call(
        norm_kernel,
        grid=(rows // block,),
        in_specs=[line, whole_spec(gain)],
        out_specs=line,
        out_shape=jax.ShapeDtypeStruct((rows, width), jnp.bfloat16),
        compiler_params=params(8),
        cost_estimate=cost(0, 8 * rows * width),
        name="norm",
    )(inputs, gain)


def outward_kernel(shares, *refs):
    context_refs, weight_refs = refs[:shares], refs[shares : 2 * shares]
    input_ref, gain_ref, hidden_ref, second_ref = refs[2 * shares :]
    total = input_ref[...]
    for context_ref, weight_ref in zip(context_refs, weight_refs):
        total = total + mm(context_ref[...], weight_ref[...])
    hidden_ref[...] = total

    def work(rows):
        normal = standard(hidden_ref[rows, :])[0]
        second_ref[rows, :] = (normal * gain_ref[...]).astype(jnp.bfloat16)

    by_rows(input_ref.shape[0], work)


def outward(contexts, weights, inputs, gain):
    rows, width = inputs.shape
    block = row_block(rows, 400)
    line = pl.BlockSpec((block, width), lambda at: (at, 0))
    gain = gain[None]
    heads = contexts[0].shape[1]
    return pl.pallas_call(
        partial(outward_kernel, len(contexts)),
        grid=(rows // block,),
        in_specs=[pl.BlockSpec((block, heads), lambda at: (at, 0))] * len(contexts)
        + [whole_spec(weight) for weight in weights]
        + [line, whole_spec(gain)],
        out_specs=[line, line],
        out_shape=[
            jax.ShapeDtypeStruct((rows, width), jnp.float32),
            jax.ShapeDtypeStruct((rows, width), jnp.bfloat16),
        ],
        compiler_params=params(16),
        cost_estimate=cost(4 * rows * width * width, 12 * rows * width),
        name="outward",
    )(*contexts, *weights, inputs, gain)


def ff_kernel(shares, per, *refs):
    second_ref, hidden_ref = refs[:2]
    up_refs, down_refs = refs[2 : 2 + shares], refs[2 + shares : 2 + 2 * shares]
    result_ref = refs[2 + 2 * shares]
    active_refs, slope_refs = refs[3 + 2 * shares : 3 + 3 * shares], refs[3 + 3 * shares :]
    chunk = pl.program_id(1)

    @pl.when(chunk == 0)
    def _():
        result_ref[...] = hidden_ref[...]

    for share in range(shares):

        @pl.when((chunk >= share * per) & (chunk < (share + 1) * per))
        def _():
            ranges = spans(second_ref.shape[0], 272)
            up, down = up_refs[share][...], down_refs[share][...]
            ahead = mm(second_ref[ranges[0][0] : ranges[0][1], :], up)
            for at, (start, end) in enumerate(ranges):
                upward = ahead
                if at + 1 < len(ranges):
                    ahead = mm(second_ref[ranges[at + 1][0] : ranges[at + 1][1], :], up)
                active, slope = gelu_pair(upward)
                active_refs[share][start:end, :] = active
                slope_refs[share][start:end, :] = slope
                result_ref[start:end, :] += mm(active, down)


def share_spec(block, place, share, per):
    if place == 1:
        return pl.BlockSpec(block, lambda at, chunk: (0, jnp.clip(chunk - share * per, 0, per - 1)))
    if place == 0:
        return pl.BlockSpec(block, lambda at, chunk: (jnp.clip(chunk - share * per, 0, per - 1), 0))
    return pl.BlockSpec(block, lambda at, chunk: (at, jnp.clip(chunk - share * per, 0, per - 1)))


def ff_sizes(rows, ups, most):
    block = rows // 2 if rows % 32 == 0 and rows > 1024 else rows
    width, units = ups[0].shape
    size = min(most if rows > 128 else 1024, units)
    return block, width, units, size, units // size


def feed(second, hidden, ups, downs):
    rows, shares = second.shape[0], len(ups)
    block, width, units, size, per = ff_sizes(rows, ups, 512)
    line = pl.BlockSpec((block, width), lambda at, chunk: (at, 0))
    piece = [share_spec((block, size), 2, share, per) for share in range(shares)]
    out = pl.pallas_call(
        partial(ff_kernel, shares, per),
        grid=(rows // block, shares * per),
        in_specs=[line, line]
        + [share_spec((width, size), 1, share, per) for share in range(shares)]
        + [share_spec((size, width), 0, share, per) for share in range(shares)],
        out_specs=[line] + piece + piece,
        out_shape=[jax.ShapeDtypeStruct((rows, width), jnp.float32)]
        + [jax.ShapeDtypeStruct((rows, units), jnp.bfloat16)] * (2 * shares),
        compiler_params=params(56),
        cost_estimate=cost(5 * rows * width * units * shares * (rows > 128), 20 * rows * width),
        name="feed",
    )(second, hidden, *ups, *downs)
    return out[0], out[1 : 1 + shares], out[1 + shares :]


def ff_back_kernel(shares, per, *refs):
    grad_ref, hidden_ref, gain_ref = refs[:3]
    slope_refs = refs[3 : 3 + shares]
    up_refs, down_refs = refs[3 + shares : 3 + 2 * shares], refs[3 + 2 * shares : 3 + 3 * shares]
    mixed_ref, branch_ref, low_ref, gain_grad_ref = refs[3 + 3 * shares : 7 + 3 * shares]
    inner_refs = refs[7 + 3 * shares :]
    block, chunk = pl.program_id(0), pl.program_id(1)

    @pl.when(chunk == 0)
    def _():
        low_ref[...] = grad_ref[...].astype(jnp.bfloat16)
        mixed_ref[...] = jnp.zeros_like(mixed_ref)

    @pl.when((block == 0) & (chunk == 0))
    def _():
        gain_grad_ref[...] = jnp.zeros_like(gain_grad_ref)

    for share in range(shares):

        @pl.when((chunk >= share * per) & (chunk < (share + 1) * per))
        def _():
            ranges = spans(grad_ref.shape[0], 800)
            up, down = up_refs[share][...], down_refs[share][...]
            ahead = nt(low_ref[ranges[0][0] : ranges[0][1], :], down)
            for at, (start, end) in enumerate(ranges):
                grad_active = ahead
                if at + 1 < len(ranges):
                    ahead = nt(low_ref[ranges[at + 1][0] : ranges[at + 1][1], :], down)
                slope = slope_refs[share][start:end, :].astype(jnp.float32)
                inner = (grad_active * slope).astype(jnp.bfloat16)
                inner_refs[share][start:end, :] = inner
                mixed_ref[start:end, :] += nt(inner, up)

    @pl.when(chunk == shares * per - 1)
    def _():
        def work(rows):
            normal, inverse = standard(hidden_ref[rows, :])
            back, gain_grad = standard_back(mixed_ref[rows, :], normal, inverse, gain_ref[...])
            total = grad_ref[rows, :] + back
            mixed_ref[rows, :] = total
            branch_ref[rows, :] = total.astype(jnp.bfloat16)
            gain_grad_ref[...] += gain_grad

        by_rows(grad_ref.shape[0], work)


def feed_back(grad, hidden, gain, slopes, ups, downs):
    rows, shares = grad.shape[0], len(ups)
    block, width, units, size, per = ff_sizes(rows, ups, 512)
    line = pl.BlockSpec((block, width), lambda at, chunk: (at, 0))
    gain = gain[None]
    piece = [share_spec((block, size), 2, share, per) for share in range(shares)]
    out = pl.pallas_call(
        partial(ff_back_kernel, shares, per),
        grid=(rows // block, shares * per),
        in_specs=[line, line, whole_spec(gain)]
        + piece
        + [share_spec((width, size), 1, share, per) for share in range(shares)]
        + [share_spec((size, width), 0, share, per) for share in range(shares)],
        out_specs=[line, line, line, eight_spec(width)] + piece,
        out_shape=[
            jax.ShapeDtypeStruct((rows, width), jnp.float32),
            jax.ShapeDtypeStruct((rows, width), jnp.bfloat16),
            jax.ShapeDtypeStruct((rows, width), jnp.bfloat16),
            jax.ShapeDtypeStruct((8, width), jnp.float32),
        ]
        + [jax.ShapeDtypeStruct((rows, units), jnp.bfloat16)] * shares,
        compiler_params=params(50),
        cost_estimate=light(),
        name="feed_back",
    )(grad, hidden, gain, *slopes, *ups, *downs)
    return out[0], out[1], out[2], jnp.sum(out[3], axis=0), out[4:]


def split(value):
    high = value.astype(jnp.bfloat16)
    return high, (value - high.astype(jnp.float32)).astype(jnp.bfloat16)


def learn_kernel(bias_ref, input_ref, gain_ref, maps_ref, tokens_ref, shares_ref, high, low_part):
    def work(rows):
        high[rows, :], low_part[rows, :] = split(standard(input_ref[rows, :])[0])

    by_eights(input_ref.shape[0], work)
    maps = jnp.concatenate(split(maps_ref[...] * gain_ref[...]))
    logits = nt(maps, high[...])
    logits = logits[:S] + logits[S:] + nt(maps[:S], low_part[...])
    logits = jnp.concatenate([logits] * (bias_ref.shape[1] // S), axis=0) + bias_ref[0]
    weights = jnp.exp(logits - jnp.max(logits, axis=-1, keepdims=True))
    shares = weights / jnp.sum(weights, axis=-1, keepdims=True)
    shares_ref[0] = shares

    def cut(rows):
        high[rows, :], low_part[rows, :] = split(input_ref[rows, :])

    by_eights(input_ref.shape[0], cut)
    both = jnp.concatenate(split(shares))
    tokens, count = mm(both, high[...]), shares.shape[0]
    tokens_ref[...] = tokens[:count] + tokens[count:] + mm(both[:count], low_part[...])


def by_eights(rows, work):
    for at in range(0, rows, 112):
        work(pl.ds(at, min(112, rows - at)))


def pair_bias(keep):
    step = 4 if keep.shape[0] % 4 == 0 else 2
    seen = keep.reshape(-1, 1, step * P_SIZE)
    own = (jnp.arange(step * S)[:, None] // S) == (jnp.arange(step * P_SIZE)[None] // P_SIZE)
    return jnp.where(seen & own[None], 0.0, -1e30).astype(jnp.float32)


def learn(bias, patched, gain, maps):
    rows, width = patched.shape
    steps, count, span = bias.shape
    gain = gain[None]
    line = pl.BlockSpec((span, width), lambda at: (at, 0))
    mark = pl.BlockSpec((1, count, span), lambda at: (at, 0, 0))
    return pl.pallas_call(
        learn_kernel,
        grid=(steps,),
        in_specs=[mark, line, whole_spec(gain), whole_spec(maps)],
        out_specs=[pl.BlockSpec((count, width), lambda at: (at, 0)), mark],
        out_shape=[
            jax.ShapeDtypeStruct((steps * count, width), jnp.float32),
            jax.ShapeDtypeStruct(bias.shape, jnp.float32),
        ],
        scratch_shapes=[pltpu.VMEM((span, width), jnp.bfloat16)] * 2,
        compiler_params=params(24),
        cost_estimate=cost(0, 12 * rows * width),
        name="learn",
    )(bias, patched, gain, maps)


def outer(left, right):
    (left_high, left_low), (right_high, right_low) = split(left), split(right)
    return tn(
        jnp.concatenate((left_high, left_high, left_low)),
        jnp.concatenate((right_high, right_low, right_high)),
    )


def learn_back_kernel(
    shares_ref, grad_ref, input_ref, gain_ref, maps_ref,
    out_ref, low_ref, gain_grad_ref, maps_grad_ref, high, low_part, inverses, slope,
):
    @pl.when(pl.program_id(0) == 0)
    def _():
        gain_grad_ref[...] = jnp.zeros_like(gain_grad_ref)
        maps_grad_ref[...] = jnp.zeros_like(maps_grad_ref)

    def cut(rows):
        high[rows, :], low_part[rows, :] = split(input_ref[rows, :])

    by_eights(input_ref.shape[0], cut)
    shares, grad = shares_ref[0], grad_ref[...]
    both = jnp.concatenate(split(grad))
    product, count = nt(both, high[...]), shares.shape[0]
    product = product[:count] + product[count:] + nt(both[:count], low_part[...])
    product = shares * product
    logits = product - shares * jnp.sum(product, axis=-1, keepdims=True)
    logits = sum(logits[at : at + S] for at in range(S, count, S)) + logits[:S]
    slope[...] = outer(logits, maps_ref[...])
    out_ref[...] = outer(shares, grad)

    def before(rows):
        normal, inverse = standard(input_ref[rows, :])
        high[rows, :], low_part[rows, :] = split(normal)
        inverses[rows, :] = jnp.broadcast_to(inverse, inverses[rows, :].shape)

    by_eights(input_ref.shape[0], before)
    both = jnp.concatenate(split(logits))
    maps_grad = mm(both, high[...])
    maps_grad = maps_grad[:S] + maps_grad[S:] + mm(both[:S], low_part[...])
    maps_grad_ref[...] += maps_grad * gain_ref[...]

    def after(rows):
        normal = high[rows, :].astype(jnp.float32) + low_part[rows, :].astype(jnp.float32)
        back, gain_grad = standard_back(
            slope[rows, :], normal, inverses[rows, 0:1], gain_ref[...]
        )
        total = out_ref[rows, :] + back
        out_ref[rows, :] = total
        low_ref[rows, :] = total.astype(jnp.bfloat16)
        gain_grad_ref[...] += gain_grad

    by_eights(input_ref.shape[0], after)


def learn_back(shares, grad, patched, gain, maps):
    rows, width = patched.shape
    steps, count, span = shares.shape
    gain = gain[None]
    line = pl.BlockSpec((span, width), lambda at: (at, 0))
    mark = pl.BlockSpec((1, count, span), lambda at: (at, 0, 0))
    out = pl.pallas_call(
        learn_back_kernel,
        grid=(steps,),
        in_specs=[
            mark,
            pl.BlockSpec((count, width), lambda at: (at, 0)),
            line,
            whole_spec(gain),
            whole_spec(maps),
        ],
        out_specs=[line, line, eight_spec(width), whole_spec(maps)],
        out_shape=[
            jax.ShapeDtypeStruct((rows, width), jnp.float32),
            jax.ShapeDtypeStruct((rows, width), jnp.bfloat16),
            jax.ShapeDtypeStruct((8, width), jnp.float32),
            jax.ShapeDtypeStruct(maps.shape, jnp.float32),
        ],
        scratch_shapes=[
            pltpu.VMEM((span, width), jnp.bfloat16),
            pltpu.VMEM((span, width), jnp.bfloat16),
            pltpu.VMEM((span, 128), jnp.float32),
            pltpu.VMEM((span, width), jnp.float32),
        ],
        compiler_params=params(36),
        cost_estimate=light(),
        name="learn_back",
    )(shares, grad, patched, gain, maps)
    return out[0], out[1], jnp.sum(out[2], axis=0), out[3]


def inward_back_kernel(shares, *refs):
    grad_refs, weight_refs = refs[:shares], refs[shares : 2 * shares]
    later_ref, input_ref, gain_ref, out_ref, gain_grad_ref = refs[2 * shares :]

    @pl.when(pl.program_id(0) == 0)
    def _():
        gain_grad_ref[...] = jnp.zeros_like(gain_grad_ref)

    total = None
    for grad_ref, weight_ref in zip(grad_refs, weight_refs):
        for at in range(3):
            term = nt(grad_ref[at], weight_ref[at])
            total = term if total is None else total + term
    out_ref[...] = total

    def work(rows):
        normal, inverse = standard(input_ref[rows, :])
        back, gain_grad = standard_back(out_ref[rows, :], normal, inverse, gain_ref[...])
        out_ref[rows, :] = later_ref[rows, :] + back
        gain_grad_ref[...] += gain_grad

    by_rows(input_ref.shape[0], work)


def inward_back(grads, weights, later, inputs, gain):
    rows, width = inputs.shape
    block = row_block(rows, 400)
    line = pl.BlockSpec((block, width), lambda at: (at, 0))
    gain = gain[None]
    heads = grads[0].shape[2]
    out = pl.pallas_call(
        partial(inward_back_kernel, len(grads)),
        grid=(rows // block,),
        in_specs=[pl.BlockSpec((3, block, heads), lambda at: (0, at, 0))] * len(grads)
        + [
            pl.BlockSpec((3, width, heads), lambda at, panel=panel: (0, 0, panel))
            for _, panel in weights
        ]
        + [line, line, whole_spec(gain)],
        out_specs=[line, eight_spec(width)],
        out_shape=[
            jax.ShapeDtypeStruct((rows, width), jnp.float32),
            jax.ShapeDtypeStruct((8, width), jnp.float32),
        ],
        compiler_params=params(28),
        cost_estimate=light(),
        name="inward_back",
    )(*grads, *(weight for weight, _ in weights), later, inputs, gain)
    return out[0], jnp.sum(out[1], axis=0)


def few_kernel(shares, *refs):
    input_ref, gain_one_ref, gain_two_ref, bias_ref = refs[:4]
    qkv_refs, out_refs = refs[4 : 4 + shares], refs[4 + shares : 4 + 2 * shares]
    across_ref, hidden_ref, second_ref = refs[4 + 2 * shares : 7 + 2 * shares]
    projected_refs = refs[7 + 2 * shares : 7 + 3 * shares]
    context_refs = refs[7 + 3 * shares :]
    total = input_ref[...]
    across = (standard(total)[0] * gain_one_ref[...]).astype(jnp.bfloat16)
    across_ref[...] = across
    for share in range(shares):
        parts = [mm(across, qkv_refs[share][at]).astype(jnp.bfloat16) for at in range(3)]
        for at, part in enumerate(parts):
            projected_refs[share][at] = part
        for first in range(0, parts[0].shape[1], 2 * HEAD_DIM):
            query, keys, values = (part[:, first : first + 2 * HEAD_DIM] for part in parts)
            context_refs[share][:, first : first + 2 * HEAD_DIM] = mix(
                scaled(query), keys, values, bias_ref[...]
            )
    for share in range(shares):
        total = total + mm(context_refs[share][...], out_refs[share][...])
    hidden_ref[...] = total
    second_ref[...] = (standard(total)[0] * gain_two_ref[...]).astype(jnp.bfloat16)


def few(inputs, gain_one, gain_two, bias, weights_qkv, weights_out):
    rows, width = inputs.shape
    shares, columns = len(weights_qkv), weights_qkv[0].shape[2]
    line = jax.ShapeDtypeStruct((rows, width), jnp.bfloat16)
    out = pl.pallas_call(
        partial(few_kernel, shares),
        out_shape=[line, jax.ShapeDtypeStruct((rows, width), jnp.float32), line]
        + [jax.ShapeDtypeStruct((3, rows, columns), jnp.bfloat16)] * shares
        + [jax.ShapeDtypeStruct((rows, columns), jnp.bfloat16)] * shares,
        compiler_params=params(28),
        cost_estimate=light(),
        name="few",
    )(inputs, gain_one[None], gain_two[None], bias, *weights_qkv, *weights_out)
    return out[0], out[1], out[2], out[3 : 3 + shares], out[3 + shares :]


def few_back_kernel(shares, *refs):
    branch_ref, later_ref, input_ref, gain_ref, bias_ref = refs[:5]
    projected_refs = refs[5 : 5 + shares]
    qkv_refs, out_refs = refs[5 + shares : 5 + 2 * shares], refs[5 + 2 * shares : 5 + 3 * shares]
    grad_ref, gain_grad_ref = refs[5 + 3 * shares : 7 + 3 * shares]
    back_refs = refs[7 + 3 * shares :]
    total = None
    for share in range(shares):
        grad = nt(branch_ref[...], out_refs[share][...]).astype(jnp.bfloat16)
        for first in range(0, grad.shape[1], 2 * HEAD_DIM):
            pair = slice(first, first + 2 * HEAD_DIM)
            query, keys, values = (projected_refs[share][at, :, pair] for at in range(3))
            parts = mix_back(scaled(query), keys, values, grad[:, pair], bias_ref[...])
            for at, part in enumerate(parts):
                back_refs[share][at, :, pair] = part
    for share in range(shares):
        for at in range(3):
            term = nt(back_refs[share][at], qkv_refs[share][at])
            total = term if total is None else total + term
    normal, inverse = standard(input_ref[...])
    back, gain_grad = standard_back(total, normal, inverse, gain_ref[...])
    grad_ref[...] = later_ref[...] + back
    gain_grad_ref[...] = gain_grad


def few_back(branch, later, inputs, gain, bias, projected, weights_qkv, weights_out):
    rows, width = inputs.shape
    shares, columns = len(weights_qkv), weights_qkv[0].shape[2]
    out = pl.pallas_call(
        partial(few_back_kernel, shares),
        out_shape=[
            jax.ShapeDtypeStruct((rows, width), jnp.float32),
            jax.ShapeDtypeStruct((8, width), jnp.float32),
        ]
        + [jax.ShapeDtypeStruct((3, rows, columns), jnp.bfloat16)] * shares,
        compiler_params=params(28),
        cost_estimate=light(),
        name="few_back",
    )(branch, later, inputs, gain[None], bias, *projected, *weights_qkv, *weights_out)
    return out[0], jnp.sum(out[1], axis=0), out[2:]


def again_kernel(rows_refs, up_ref, down_ref, up_grad_ref, down_grad_ref):
    def work(second_ref, grad_ref, begin):
        second, grad = second_ref[...], grad_ref[...]
        size = up_ref.shape[1]
        tile = min(256, size)

        def products(start):
            span = slice(start, start + tile)
            return mm(second, up_ref[:, span]), nt(grad, down_ref[span, :])

        actives, inners = [], []
        ahead = products(0)
        for start in range(0, size, tile):
            upward, grad_active = ahead
            if start + tile < size:
                ahead = products(start + tile)
            active, slope = gelu_pair(upward)
            actives.append(active)
            inners.append((grad_active * slope.astype(jnp.float32)).astype(jnp.bfloat16))
        active, inner = jnp.concatenate(actives, axis=1), jnp.concatenate(inners, axis=1)
        if begin:
            down_grad_ref[...] = tn(active, grad)
            up_grad_ref[...] = tn(second, inner)
        else:
            down_grad_ref[...] += tn(active, grad)
            up_grad_ref[...] += tn(second, inner)

    @pl.when(pl.program_id(1) == 0)
    def _():
        work(rows_refs[0], rows_refs[1], True)

    @pl.when(pl.program_id(1) == 1)
    def _():
        work(rows_refs[2], rows_refs[3], False)


def again(piece, pieces, rows, up, down, before):
    width, units = up.shape
    size = min(512, units // pieces)
    first = piece * (units // pieces // size)
    spots = [
        pl.BlockSpec((width, size), lambda chunk, part: (0, first + chunk)),
        pl.BlockSpec((size, width), lambda chunk, part: (first + chunk, 0)),
    ]

    def kernel(*refs):
        again_kernel(refs[:4], *refs[4:6], *refs[-2:])

    return pl.pallas_call(
        kernel,
        grid=(units // pieces // size, 2),
        in_specs=[whole_spec(array) for array in rows]
        + spots
        + [pl.BlockSpec(memory_space=pl.ANY)] * len(before),
        out_specs=spots,
        out_shape=[
            jax.ShapeDtypeStruct(up.shape, jnp.float32),
            jax.ShapeDtypeStruct(down.shape, jnp.float32),
        ],
        input_output_aliases={6: 0, 7: 1} if before else {},
        compiler_params=params(48),
        cost_estimate=light(),
        name="again",
    )(*rows, up, down, *before)


def swap(tensor, bit):
    count = lax.axis_size("dp")
    return lax.ppermute(tensor, "dp", [(place, place ^ (1 << bit)) for place in range(count)])


def my_bit(bit):
    return ((lax.axis_index("dp") >> bit) & 1).astype(jnp.int32).reshape(1)


def meet(value, others):
    if not others:
        return value, []
    value, others = lax.optimization_barrier((value, tuple(others)))
    return value, list(others)


def part_of(number, step, count, mine):
    first = number == mine
    return jnp.where(first, jnp.minimum(step, count - 1), jnp.maximum(step - count, 0))


def divisor(size, most):
    return max(step for step in range(16, most + 1, 16) if size % step == 0)


def fold_kernel(cuts, count, mine_ref, *refs):
    kept_ref, sent_ref = refs[-2:]
    step = pl.program_id(0)
    keep = (step < count) == (mine_ref[0] == 0)
    at = 0
    for first, last, terms in cuts:
        inside = (step >= first) & (step < last)
        sources, at = refs[at : at + terms], at + terms

        def value(sources=sources):
            total = sources[0][...].astype(jnp.float32)
            for source in sources[1:]:
                total = total + source[...].astype(jnp.float32)
            return total.astype(jnp.bfloat16)

        @pl.when(inside & keep)
        def _():
            kept_ref[...] = value()

        @pl.when(inside & jnp.logical_not(keep))
        def _():
            sent_ref[...] = value()


def fold(sources, width, mine):
    total = sum(rows for _, _, rows, _ in sources)
    block = divisor(math.gcd(total // 2, *(value for s in sources for value in s[1:3])), 512)
    count = total // 2 // block
    cuts, specs, terms, at = [], [], [], 0
    for arrays, start, rows, panel in sources:
        steps = rows // block

        def place(step, mine_ref, at=at, steps=steps, start=start // block, panel=panel):
            return start + jnp.clip(step - at, 0, steps - 1), panel

        cuts.append((at, at + steps, len(arrays)))
        specs += [pl.BlockSpec((block, width), place)] * len(arrays)
        terms += arrays
        at += steps
    half = jax.ShapeDtypeStruct((total // 2, width), jnp.bfloat16)
    return pl.pallas_call(
        partial(fold_kernel, cuts, count),
        grid_spec=pltpu.PrefetchScalarGridSpec(
            num_scalar_prefetch=1,
            grid=(2 * count,),
            in_specs=specs,
            out_specs=[
                pl.BlockSpec((block, width), lambda i, m: (part_of(m[0], i, count, 0), 0)),
                pl.BlockSpec((block, width), lambda i, m: (part_of(1 - m[0], i, count, 0), 0)),
            ],
        ),
        out_shape=[half, half],
        compiler_params=params(18),
        cost_estimate=light(),
        name="fold",
    )(mine, *terms)


def put(out_ref, value):
    value = value.astype(out_ref.dtype)
    if len(out_ref.shape) == 2:
        out_ref[...] = value
        return
    wide = out_ref.shape[2]
    for at in range(3):
        out_ref[at] = value[:, at * wide : (at + 1) * wide]


def spread_kernel(cuts, parts, mines_ref, *refs):
    outs = refs[2 * len(parts) :]
    step = pl.program_id(0)
    for at, (begin, count) in enumerate(parts):
        own_ref, got_ref = refs[2 * at : 2 * at + 2]
        own = (step < begin + count) == (mines_ref[at] == 0)
        for first, last, out in cuts[at]:
            inside = (step >= first) & (step < last)

            @pl.when(inside & own)
            def _():
                put(outs[out], own_ref[...])

            @pl.when(inside & jnp.logical_not(own))
            def _():
                put(outs[out], got_ref[...])


def spread(pieces, layouts, outs, dtype):
    width = pieces[0][0].shape[1]
    sizes = [piece[0].shape[0] for piece in pieces]
    sizes += [value for layout in layouts for entry in layout for value in entry[1:3]]
    block = divisor(math.gcd(*sizes), 512)
    parts, cuts, specs, terms, step = [], [], [], [], 0
    visits = [[] for _ in outs]
    for at, (own, got, _) in enumerate(pieces):
        count = own.shape[0] // block
        parts.append((step, count))
        for half in range(2):

            def place(i, m, at=at, half=half, begin=step, count=count):
                i = jnp.clip(i - begin, 0, 2 * count - 1)
                return part_of(m[at] if half == 0 else 1 - m[at], i, count, 0), 0

            specs.append(pl.BlockSpec((block, width), place))
        terms += [own, got]
        mine, first = [], step
        for out, start, rows, panel in layouts[at]:
            steps = rows // block
            mine.append((first, first + steps, out))
            visits[out].append((first, steps, start // block, panel))
            first += steps
        cuts.append(mine)
        step += 2 * count

    def out_spec(seen, shape):
        def place(i, m):
            row, panel = seen[0][2], seen[0][3]
            for first, steps, start, column in seen:
                here = i >= first
                row = jnp.where(here, start + jnp.clip(i - first, 0, steps - 1), row)
                panel = jnp.where(here, column, panel)
            return (row, panel) if len(shape) == 2 else (0, row, panel)

        if len(shape) == 3:
            return pl.BlockSpec((3, block, width // 3), place)
        return pl.BlockSpec((block, width), place)

    return pl.pallas_call(
        partial(spread_kernel, cuts, parts),
        grid_spec=pltpu.PrefetchScalarGridSpec(
            num_scalar_prefetch=1,
            grid=(step,),
            in_specs=specs,
            out_specs=[out_spec(seen, shape) for seen, shape in zip(visits, outs)],
        ),
        out_shape=[jax.ShapeDtypeStruct(shape, dtype) for shape in outs],
        compiler_params=params(22),
        cost_estimate=light(),
        name="spread",
    )(jnp.concatenate([mine for _, _, mine in pieces]), *terms)


def join(own, got, mine):
    rows, width = own.shape
    layout = [(0, 0, 2 * rows, 0)]
    return spread([(own, got, mine)], [layout], [(2 * rows, width)], own.dtype)[0]


class Flow:
    def __init__(self, halves, order, back=False):
        self.order, self.step = order, 0
        self.kept, self.sent = halves
        self.got = swap(self.sent, order[0])
        self.length = 2 * len(order) - 1 if back else len(order)

    def done(self):
        return self.step == self.length

    def advance(self):
        self.step += 1
        bits, turn = self.order, len(self.order)
        if self.step < turn:
            rows, width = self.kept.shape
            bit = bits[self.step]
            self.kept, self.sent = fold([((self.kept, self.got), 0, rows, 0)], width, my_bit(bit))
        elif self.step == turn:
            bit = bits[-1]
            total = self.kept.astype(jnp.float32) + self.got.astype(jnp.float32)
            self.kept = self.sent = total.astype(jnp.bfloat16)
        else:
            bit = bits[2 * turn - 1 - self.step]
            self.kept = self.sent = join(self.kept, self.got, my_bit(bits[2 * turn - self.step]))
        if self.step < self.length or self.length > turn:
            self.got = swap(self.sent, bit)


class Gather:
    def __init__(self, rows):
        self.step, self.length = 0, lax.axis_size("dp").bit_length()
        self.kept = self.sent = rows
        self.got = swap(rows, 0)

    def done(self):
        return self.step == self.length

    def advance(self):
        self.step += 1
        if self.step < self.length:
            self.kept = self.sent = join(self.kept, self.got, my_bit(self.step - 1))
            last = self.step == self.length - 1
            self.got = near(1)(self.kept) if last else swap(self.kept, self.step)


class Small:
    def __init__(self, tensors):
        self.kept = self.sent = jnp.concatenate(tensors)
        self.step, self.length = 0, lax.axis_size("mp") - 1
        self.length += lax.axis_size("dp").bit_length() - 1
        self.mine = self.kept
        self.issue()

    def issue(self):
        near_by = lax.axis_size("mp") - 1
        if self.step < near_by:
            self.got = give(self.step + 1)(self.mine)
        else:
            self.got = swap(self.kept, self.length - 1 - self.step)

    def done(self):
        return self.step == self.length

    def advance(self):
        self.kept = self.sent = self.kept + self.got
        self.step += 1
        if not self.done():
            self.issue()


class Clock:
    def __init__(self, plan):
        self.plan = plan
        self.flows, self.begun, self.past, self.whole = {}, [], [], {}

    def begin(self, name, flow):
        self.flows[name] = flow
        self.begun.append(flow.sent)

    def __call__(self, name, value):
        names = self.plan.get(name, ())
        flows = [self.flows[flow] for flow in names if flow in self.flows]
        ended = [flow for flow in flows if flow.done()]
        flows = [flow for flow in flows if not flow.done()]
        ready = [key for key in names if key in self.whole]
        waited = [flow.got for flow in flows] + [self.whole[key] for key in ready]
        waited += [flow.got for flow in ended]
        value, got = meet(value, waited + self.past)
        self.past = []
        for flow in flows:
            flow.got = got.pop(0)
            flow.advance()
        for key in ready:
            self.whole[key] = got.pop(0)
        for flow in ended:
            flow.got = got.pop(0)
        value = meet(value, self.begun + [flow.sent for flow in flows])[0]
        self.begun = []
        return value

    def end(self, names):
        flows = [self.flows[name] for name in names]
        while not all(flow.done() for flow in flows):
            for flow in flows:
                if not flow.done():
                    flow.advance()


def grads_kernel(cuts, count, *refs):
    outs = refs[-2:] if count else refs[-1:]
    step = pl.program_id(0)
    keep = True if not count else (step < count) == (refs[0][0] == 0)
    at = 1
    for first, last, terms in cuts:
        inside = (step >= first) & (step < last)
        sources, at = refs[at : at + terms], at + terms

        @pl.when(inside)
        def _(sources=sources):
            if len(sources[1].shape) == 2:
                total = tn(sources[0][...], sources[1][...])
            else:
                left = sources[0][...].T
                total = jnp.concatenate([mm(left, sources[1][part]) for part in range(3)], axis=1)
            if len(sources) > 2:
                total = total + sources[2][...].astype(jnp.float32)
            total = total.astype(jnp.bfloat16)
            if not count:
                outs[0][...] = total
                return

            @pl.when(keep)
            def _():
                outs[0][...] = total

            @pl.when(jnp.logical_not(keep))
            def _():
                outs[1][...] = total


def grads(sources, width, mine=None):
    total = sum(source[2] for source in sources)
    sizes = [value for source in sources for value in source[1:3]]
    if mine is not None:
        sizes.append(total // 2)
    sizes += [source[6] for source in sources if len(source) > 5]
    block = divisor(math.gcd(*sizes), 512)
    cuts, specs, terms, at = [], [], [], 0
    for source in sources:
        left, start, columns, right, panel = source[:5]
        steps = columns // block
        rows = left.shape[0]

        def here(step, at=at, steps=steps):
            return jnp.clip(step - at, 0, steps - 1)

        specs.append(
            pl.BlockSpec((rows, block), lambda i, *m, f=here, s=start // block: (0, s + f(i)))
        )
        if right.ndim == 2:
            specs.append(pl.BlockSpec((rows, width), lambda i, *m, p=panel: (0, p)))
        else:
            specs.append(whole_spec(right))
        terms += [left, right]
        if len(source) > 5:
            other, row, column = source[5:]
            specs.append(
                pl.BlockSpec(
                    (block, width), lambda i, *m, f=here, s=row // block, p=column: (s + f(i), p)
                )
            )
            terms.append(other)
        cuts.append((at, at + steps, 3 if len(source) > 5 else 2))
        at += steps
    count = 0 if mine is None else total // 2 // block
    if count:
        shape = jax.ShapeDtypeStruct((total // 2, width), jnp.bfloat16)
        out_shape = [shape, shape]
        out_specs = [
            pl.BlockSpec((block, width), lambda i, m: (part_of(m[0], i, count, 0), 0)),
            pl.BlockSpec((block, width), lambda i, m: (part_of(1 - m[0], i, count, 0), 0)),
        ]
    else:
        mine = jnp.zeros((1,), jnp.int32)
        out_shape = jax.ShapeDtypeStruct((total, width), jnp.bfloat16)
        out_specs = pl.BlockSpec((block, width), lambda i, m: (i, 0))
    return pl.pallas_call(
        partial(grads_kernel, cuts, count),
        grid_spec=pltpu.PrefetchScalarGridSpec(
            num_scalar_prefetch=1, grid=(at,), in_specs=specs, out_specs=out_specs
        ),
        out_shape=out_shape,
        compiler_params=params(38),
        cost_estimate=light(),
        name="grads",
    )(mine, *terms)


def near(step):
    count = lax.axis_size("mp")
    pairs = [((to + step) % count, to) for to in range(count)]
    return lambda tensor: lax.ppermute(tensor, "mp", pairs)


def give(step):
    count = lax.axis_size("mp")
    pairs = [(start, (start + step) % count) for start in range(count)]
    return lambda tensor: lax.ppermute(tensor, "mp", pairs)


def fetch(tensor):
    return [tensor] + [near(step)(tensor) for step in range(1, lax.axis_size("mp"))]


def total_over_all(terms):
    total = terms[0].astype(jnp.float32)
    for step in range(1, len(terms)):
        total = total + give(step)(terms[step]).astype(jnp.float32)
    return lax.psum(total.astype(jnp.bfloat16), "dp").astype(jnp.float32)


def lower_forward(inputs, weights, bias, later):
    gain_one, weight_qkv, weight_out, gain_two, weight_up, weight_down = weights
    across = norm(inputs, gain_one)
    projections, contexts = [], []
    for share in weight_qkv:
        projected = jnp.einsum(
            "rd,tdc->trc", across, share, preferred_element_type=jnp.float32
        ).astype(jnp.bfloat16)
        projections.append(projected)
        contexts.append(attend(bias, projected))
    hidden, second = outward(contexts, weight_out, inputs, gain_two)
    second, later = meet(second, later)
    result, actives, slopes = feed(second, hidden, weight_up, weight_down)
    stored = (inputs, hidden, across, second, projections, contexts, actives, slopes)
    return result, stored, later


def upper_forward(inputs, weights, bias, clock):
    gain_one, weight_qkv, weight_out, gain_two, weight_up, weight_down = weights
    across, hidden, second, projections, contexts = few(
        inputs, gain_one, gain_two, bias, weight_qkv, weight_out
    )
    if len(weight_qkv) == 2 and lax.axis_size("dp") == 16:
        clock.begin("seconds", Gather(second))
    second = clock("second-feed", second)
    result, actives, slopes = feed(second, hidden, weight_up, weight_down)
    return result, (inputs, hidden, across, second, projections, contexts, actives, slopes)


def low(value):
    return value.astype(jnp.bfloat16)


def project_sources(across, back, others=None):
    source = (across, 0, across.shape[1], back, 0)
    return [source if others is None else source + (others, 0, 0)]


def out_sources(context, grad_branch, wide, others=None, first=0):
    rows = context.shape[1]
    panels = range(grad_branch.shape[1] // wide)
    sources = [(context, 0, rows, grad_branch, panel) for panel in panels]
    if others is None:
        return sources
    return [source + (others, first + at * rows, 0) for at, source in enumerate(sources)]


def upper_backward(grad_out, stored, weights, bias, clock):
    gain_one, weight_qkv, weight_out, gain_two, weight_up, weight_down = weights
    inputs, hidden, across, second, projections, contexts, actives, slopes = stored
    shares = range(len(weight_qkv))
    grad_out = clock("second-back", grad_out)
    grad_hidden, grad_branch, grad_mix, grad_gain_two, inners = feed_back(
        grad_out, hidden, gain_two, slopes, weight_up, weight_down
    )
    quick = len(shares) == 2 and lax.axis_size("dp") == 16
    grad_branch = clock("second-few", grad_branch)
    grad_inputs, grad_gain_one, backs = few_back(
        grad_branch, grad_hidden, inputs, gain_one, bias, projections, weight_qkv, weight_out
    )
    if quick:
        projects = grads(project_sources(across, backs[1]), 3 * contexts[0].shape[1])
        clock.past.append(projects)
        weight_grads = (across, backs, contexts, grad_branch, give(1)(projects))
    else:
        weight_grads = plain_grads(
            across, backs, contexts, grad_branch, second, inners, actives, grad_mix
        )
    return grad_inputs, grad_gain_one, grad_gain_two, weight_grads


def plain_grads(across, backs, contexts, grad_branch, second, inners, actives, grad_mix):
    shares = range(len(contexts))
    pairs = (
        [jnp.concatenate([tn(across, part) for part in backs[at]]) for at in shares],
        [tn(contexts[at], grad_branch) for at in shares],
        [tn(second, inners[at]) for at in shares],
        [tn(actives[at], grad_mix) for at in shares],
    )
    return tuple(total_over_all([low(term) for term in terms]) for terms in pairs)


def lower_backward(
    grad_out, grad_mix, stored, weights, bias, clock, upper_sources, between
):
    gain_one, weight_qkv, weight_out, gain_two, weight_up, weight_down = weights
    inputs, hidden, across, second, projections, contexts, actives, slopes = stored
    shares = range(len(weight_qkv))
    quick = len(shares) == 2 and lax.axis_size("dp") == 16
    bits = tuple(range(lax.axis_size("dp").bit_length() - 1))
    turned = (1, 0) + bits[2:]
    width, units = weight_up[0].shape
    wide = contexts[0].shape[1]
    if quick:
        upper_across, upper_backs, upper_contexts, upper_branch, project_others = upper_sources
        grad_mix, (project_others,) = meet(clock("down1", grad_mix), [project_others])
        heads = 3 * wide
        sources = [(actives[1], 0, units, grad_mix, 0)]
        others = grads(sources + out_sources(upper_contexts[1], upper_branch, width), width)
        upper_across = meet(upper_across, [others])[0]
        others = give(1)(others)
        sources = project_sources(upper_across, upper_backs[0], project_others)
        halves = grads(sources, heads, my_bit(bits[0]))
        clock.begin("heads", Flow(halves, bits, True))
        grad_mix = meet(grad_mix, halves)[0]
        sources = [(actives[0], 0, units, grad_mix, 0, others, 0, 0)]
        sources += out_sources(upper_contexts[0], upper_branch, width, others, units)
        clock.begin("down", Flow(grads(sources, width, my_bit(turned[0])), turned, True))
    grad_out = clock("feed", grad_out)
    grad_hidden, grad_branch, grad_mix, grad_gain_two, inners = feed_back(
        grad_out, hidden, gain_two, slopes, weight_up, weight_down
    )
    if quick:
        panels = range(units // width)
        grad_branch = clock("up1", grad_branch)
        sources = [(second, 0, width, inners[1], panel) for panel in panels]
        sources += out_sources(contexts[1], grad_branch, width)
        up_others = grads(sources, width)
        grad_branch = meet(grad_branch, [up_others])[0]
        up_others = give(1)(up_others)
    groups = 2 if quick and wide % (4 * HEAD_DIM) == 0 else 1
    backs, grad_contexts = {}, {}
    for group in range(groups):
        for at in reversed(shares):
            if group == 0:
                grad_branch = clock(f"heads{group}{at}", grad_branch)
                grad_contexts[at] = low(nt(grad_branch, weight_out[at]))
            else:
                grad_contexts[at] = clock(f"heads{group}{at}", grad_contexts[at])
            back = attend_back(bias, projections[at], grad_contexts[at], group, groups)
            backs[at, group] = back = clock(f"project{group}{at}", back)
            if quick and at:
                others = grads(project_sources(across, back), 3 * wide // groups)
                clock.past.append(others)
                others = give(at)(others)
            elif quick:
                sources = project_sources(across, back, others)
                halves = grads(sources, 3 * wide // groups, my_bit(bits[0]))
                clock.past += halves
                clock.begin(f"project-{group}", Flow(halves, bits, True))
                if group == 0:
                    between(clock)
            if quick and at and group == 0:
                grad_branch = clock("up0", grad_branch)
                for panel in panels:
                    sources = [
                        (second, 0, width, inners[0], panel, up_others, panel * width, 0)
                    ]
                    if panel == len(panels) - 1:
                        sources += out_sources(contexts[0], grad_branch, width, up_others, units)
                    sources[0] = (meet(second, [grad_branch])[0],) + sources[0][1:]
                    order = turned if panel % 2 else bits
                    halves = grads(sources, width, my_bit(order[0]))
                    clock.past += halves
                    clock.begin(f"up-{panel}", Flow(halves, order, True))
    weight_grads = None
    if not quick:
        whole_backs = [backs[at, 0] for at in shares]
        weight_grads = plain_grads(
            across, whole_backs, contexts, grad_branch, second, inners, actives, grad_mix
        )
    inputs = clock("inward", inputs)
    grad_inputs, grad_gain_one = inward_back(
        [backs[at, group] for at in shares for group in range(groups)],
        [(weight_qkv[at], group) for at in shares for group in range(groups)],
        grad_hidden,
        inputs,
        gain_one,
    )
    return grad_inputs, grad_gain_one, grad_gain_two, weight_grads


PLAN = {
    "learn": ("mixes",),
    "second-back": ("seconds",),
    "second-few": ("seconds",),
    "down1": ("seconds",),
    "up1": ("heads", "down", "seconds"),
    "up0": ("heads", "down", "seconds"),
    "heads00": ("heads", "down"),
    "again0": ("heads", "down"),
    "heads11": ("heads", "down", "up-0", "up-1", "project-0"),
    "heads10": ("heads", "down", "up-0", "up-1", "project-0"),
    "project10": ("up-0", "up-1", "project-0"),
    "inward": ("heads", "down", "up-0", "up-1"),
    "again1": ("up-0", "up-1", "project-0", "project-1"),
    "tail0": ("up-0", "up-1", "project-0", "project-1", "small"),
    "tail1": ("heads", "down", "up-0", "up-1", "project-0", "project-1", "small"),
    "tail2": ("project-0", "project-1", "small"),
    "tail3": ("project-1",),
    "tail4": ("up-0", "up-1", "project-1", "small"),
    "tail5": ("project-0", "project-1", "small"),
}


def again_part(clock, piece, token_up, token_down):
    if piece == 0:
        seconds, mixes = clock.flows["seconds"], clock.whole["mixes"]
        clock.rows = [seconds.kept, mixes, seconds.got, near(1)(mixes)]
        clock.ready = ()
    clock.rows[0] = clock(f"again{piece}", clock.rows[0])
    clock.ready = again(piece, 2, clock.rows, token_up, token_down, clock.ready)
    clock.past += clock.ready


def finish(clock, input_grad, project, out, up, down, token_up, token_down):
    width, wide, units = project.shape[1], project.shape[2], up.shape[1]
    wider = jnp.float32
    clock.past.append(input_grad)
    again_part(clock, 1, token_up, token_down)
    token_upward_grad, token_downward_grad = clock.ready

    def last(name):
        flow = clock.flows[name]
        return flow.kept, flow.got, my_bit(flow.order[0])

    def tail(number, value):
        value = clock(f"tail{number}", value)
        clock.past.append(value)
        return value

    token_downward_grad = tail(0, token_downward_grad)
    token_downward_grad = tail(1, token_downward_grad)
    patch_downward_grad, token_outproj_grad = spread(
        [last("down")], [[(0, 0, units, 0), (1, 0, wide, 0)]], [down.shape, out.shape], wider
    )
    patch_downward_grad = tail(2, patch_downward_grad)
    (token_project_grad,) = spread([last("heads")], [[(0, 0, width, 0)]], [project.shape], wider)
    token_project_grad = tail(3, token_project_grad)
    token_project_grad = tail(4, token_project_grad)
    ups = range(units // width)
    layouts = [[(0, 0, width, panel)] for panel in ups]
    layouts[-1].append((1, 0, wide, 0))
    patch_upward_grad, patch_outproj_grad = spread(
        [last(f"up-{panel}") for panel in ups], layouts, [up.shape, out.shape], wider
    )
    patch_upward_grad = tail(5, patch_upward_grad)
    clock.end(clock.flows)
    (patch_project_grad,) = spread(
        [last("project-0"), last("project-1")],
        [[(0, 0, width, 0)], [(0, 0, width, 1)]],
        [project.shape],
        wider,
    )
    return (
        (token_project_grad, token_outproj_grad, token_upward_grad, token_downward_grad),
        (patch_project_grad, patch_outproj_grad, patch_upward_grad, patch_downward_grad),
    )


def local(
    inputs,
    patch_keep,
    patch_gainone,
    patch_project,
    patch_outproj,
    patch_gaintwo,
    patch_upward,
    patch_downward,
    learner_gain,
    learner_weight,
    token_gainone,
    token_project,
    token_outproj,
    token_gaintwo,
    token_upward,
    token_downward,
    output_grad,
):
    shards = lax.axis_size("mp")
    images_here = patch_keep.shape[0] // shards
    local_keep = (
        lax.dynamic_slice_in_dim(patch_keep, lax.axis_index("mp") * images_here, images_here, 0) > 0
    )
    lower_params = (
        patch_gainone,
        fetch(patch_project),
        fetch(patch_outproj),
        patch_gaintwo,
        fetch(patch_upward),
        fetch(patch_downward),
    )
    lower_bias = key_bias(local_keep)
    image = jnp.arange(images_here * S) // S
    upper_bias = jnp.where(image[:, None] == image[None], 0.0, -1e30).astype(jnp.float32)
    token_weights = [token_project, token_outproj, token_upward, token_downward]
    patched, lower_stored, token_weights = lower_forward(
        inputs, lower_params, lower_bias, token_weights
    )
    weight_qkv, weight_out, weight_up, weight_down = (fetch(weight) for weight in token_weights)
    upper_params = (token_gainone, weight_qkv, weight_out, token_gaintwo, weight_up, weight_down)
    maps = learner_weight.T
    clock = Clock(PLAN)
    if shards == 2 and lax.axis_size("dp") == 16:
        clock.whole["mixes"] = lax.all_gather(low(output_grad), "dp", tiled=True)
    patched = clock("learn", patched)
    tokens, shares = learn(pair_bias(local_keep), patched, learner_gain, maps)
    token_output, upper_stored = upper_forward(tokens, upper_params, upper_bias, clock)
    token_grad, token_gainone_grad, token_gaintwo_grad, token_grads = upper_backward(
        output_grad, upper_stored, upper_params, upper_bias, clock
    )
    patched_grad, patched_low, learner_gain_grad, maps_grad = learn_back(
        shares, clock("learner", token_grad), patched, learner_gain, maps
    )
    input_grad, patch_gainone_grad, patch_gaintwo_grad, patch_grads = lower_backward(
        patched_grad,
        patched_low,
        lower_stored,
        lower_params,
        lower_bias,
        clock,
        token_grads,
        lambda clock: again_part(clock, 0, token_upward, token_downward),
    )
    gains = (
        patch_gainone_grad,
        patch_gaintwo_grad,
        learner_gain_grad,
        token_gainone_grad,
        token_gaintwo_grad,
    )
    clock.begin("small", Small([maps_grad] + [gain[None] for gain in gains]))
    if patch_grads is None:
        token_grads, patch_grads = finish(
            clock,
            input_grad,
            patch_project,
            patch_outproj,
            patch_upward,
            patch_downward,
            token_upward,
            token_downward,
        )
    else:
        clock.end(["small"])
    small = clock.flows["small"].kept
    token_project_grad, token_outproj_grad, token_upward_grad, token_downward_grad = token_grads
    patch_project_grad, patch_outproj_grad, patch_upward_grad, patch_downward_grad = patch_grads
    return (
        token_output,
        input_grad,
        small[8],
        patch_project_grad.reshape(patch_project.shape),
        patch_outproj_grad,
        small[9],
        patch_upward_grad,
        patch_downward_grad,
        small[10],
        small[:S].T,
        small[11],
        token_project_grad.reshape(token_project.shape),
        token_outproj_grad,
        small[12],
        token_upward_grad,
        token_downward_grad,
    )


def solution(mesh):
    in_specs = (
        P(("dp", "mp"), None),
        P("dp", None),
        P(),
        P(None, None, "mp"),
        P("mp", None),
        P(),
        P(None, "mp"),
        P("mp", None),
        P(),
        P(),
        P(),
        P(None, None, "mp"),
        P("mp", None),
        P(),
        P(None, "mp"),
        P("mp", None),
        P(("dp", "mp"), None),
    )
    out_specs = (
        P(("dp", "mp"), None),
        P(("dp", "mp"), None),
        P(),
        P(None, None, "mp"),
        P("mp", None),
        P(),
        P(None, "mp"),
        P("mp", None),
        P(),
        P(),
        P(),
        P(None, None, "mp"),
        P("mp", None),
        P(),
        P(None, "mp"),
        P("mp", None),
    )
    return jax.shard_map(local, mesh=mesh, in_specs=in_specs, out_specs=out_specs, check_vma=False)
```
